256 devices in a mesh: ctx: 32 (over y, z), head: 8 (over x, core).
Axes of the slice: x: 4, y: 4, z: 8, core: 2. Of those that a mesh axis runs over, the one named last changes fastest.
Arguments:
- tokens: bfloat16 [65536, 2048], P('ctx'), may hold values from -6 to 6
- w_query: bfloat16 [2048, 2048], P(None, 'head'), may hold values from -0.125 to 0.125
- w_key: bfloat16 [2048, 2048], P(None, 'head'), may hold values from -0.125 to 0.125
- w_value: bfloat16 [2048, 2048], P(None, 'head'), may hold values from -0.125 to 0.125
- w_out: bfloat16 [2048, 2048], P('head'), may hold values from -0.125 to 0.125
- decay_rate: float32 [65536, 16], P('ctx', 'head'), may hold values from 0 to 1
- level_row_index: int32 [65536], P('ctx'), may hold values from 0 to 63
- level_weight_table: float32 [64, 16, 11], P(None, 'head'), may hold values from 0.2 to 2
Outputs:
- mixed: bfloat16 [65536, 2048], P('ctx', 'head')
The draws below stay inside these ranges and needn't reach their ends.
All inputs are finite; a program needn't handle non-finite values.
Results may differ from the reference program's by a relative error of at most 0.02.
Values may be sent and summed in bfloat16 or wider, within the bound.
A program may use at most 128 MiB of HBM per device.

```python
import math
import jax
import jax.numpy as jnp
from jax import lax

D = 2048
ATTENDER_NUMBER = 16
DH = 128
BLOCK = 64
TABLE_ROWS = 64
SEQUENCE_SPAN = 65536
HEAD_DEV = 2
LEVEL_COUNT = 11


def draw_decay_rate(key, part):
    key = jax.random.fold_in(key, 7)
    derived_prng_seeds = jax.random.split(key, 6)
    fast_share = 0.5
    quick_heads = jax.random.uniform(derived_prng_seeds[0], (ATTENDER_NUMBER,)) < fast_share
    fast_rate = jnp.exp(jax.random.uniform(derived_prng_seeds[1], (ATTENDER_NUMBER,), minval=math.log(1.0 / 50.0), maxval=math.log(1.0 / 30.0)))
    slow_rate = jax.random.uniform(derived_prng_seeds[2], (ATTENDER_NUMBER,), minval=0.2, maxval=0.8) / SEQUENCE_SPAN
    resting_decay_speed = jnp.where(quick_heads, fast_rate, slow_rate)
    perturbation_scale = jnp.exp(jax.random.uniform(derived_prng_seeds[3], (SEQUENCE_SPAN, ATTENDER_NUMBER), minval=math.log(0.5), maxval=math.log(2.0)))
    spike_extent = jax.random.uniform(derived_prng_seeds[5], (SEQUENCE_SPAN, ATTENDER_NUMBER), minval=0.2, maxval=0.4)
    spike_clusters = jnp.where(jax.random.uniform(derived_prng_seeds[4], (SEQUENCE_SPAN, ATTENDER_NUMBER)) < 3.0 / SEQUENCE_SPAN, spike_extent, 0.0)
    return (resting_decay_speed[None, :] * perturbation_scale + spike_clusters).astype(jnp.float32)


def with_ends(entries, key, smallest, top_value):
    place = [jax.random.randint(jax.random.fold_in(key, axis), (), 0, length) for axis, length in enumerate(entries.shape)]
    widest = entries.shape.index(max(entries.shape))
    neighbour = place[:widest] + [(place[widest] + 1) % entries.shape[widest]] + place[widest + 1:]
    return entries.at[tuple(place)].set(smallest).at[tuple(neighbour)].set(top_value)


def block_scale(rng, shape, pieces, low, largest):
    loudness, own = 1.0, jax.random.fold_in(rng, 6)
    for axis_at, blocks in pieces:
        steps = jnp.exp(jax.random.uniform(jax.random.fold_in(own, axis_at), (blocks,), jnp.float32, low / len(pieces), largest / len(pieces)))
        loudness = loudness * jnp.repeat(steps, shape[axis_at] // blocks).reshape([-1 if axis == axis_at else 1 for axis in range(len(shape))])
    return loudness


def centred(rng, shape, scale, most, shards=(), kind=jnp.bfloat16):
    factor_of = block_scale(rng, shape, shards, -0.22, 0.18) if shards else 1.0
    entries = jax.random.normal(rng, shape, jnp.float32) * scale * factor_of
    return jnp.minimum(jnp.maximum(entries, -most), most).astype(kind)


def setup_inputs(seed: int = 0) -> dict:
    streams_of = jax.random.split(jax.random.key(seed), 9)
    tokens = centred(streams_of[0], (SEQUENCE_SPAN, D), 1.0, 6.0, ((0, 32),))
    w_query = centred(streams_of[1], (D, ATTENDER_NUMBER * DH), D ** -0.5, 0.125, ((1, 8),))
    w_key = centred(streams_of[2], (D, ATTENDER_NUMBER * DH), D ** -0.5, 0.125, ((1, 8),))
    w_value = centred(streams_of[3], (D, ATTENDER_NUMBER * DH), D ** -0.5, 0.125, ((1, 8),))
    w_out = centred(streams_of[4], (ATTENDER_NUMBER * DH, D), (ATTENDER_NUMBER * DH) ** -0.5, 0.125, ((0, 8),))
    decay_rate = draw_decay_rate(jax.random.fold_in(streams_of[8], 71), 0)
    level_row_index = with_ends(jax.random.randint(streams_of[6], (SEQUENCE_SPAN,), 0, TABLE_ROWS), jax.random.fold_in(streams_of[6], 1), 0, TABLE_ROWS - 1).astype(jnp.int32)
    level_weight_table = jnp.clip(jnp.exp(math.log(2.0) - 2.3025851 * jax.random.uniform(streams_of[7], (TABLE_ROWS, ATTENDER_NUMBER, LEVEL_COUNT), jnp.float32) ** block_scale(streams_of[7], (TABLE_ROWS, ATTENDER_NUMBER, LEVEL_COUNT), ((1, 8),), -0.2, 0.2)), 0.2, 2.0)
    return dict(tokens=tokens, w_query=w_query, w_key=w_key, w_value=w_value, w_out=w_out, decay_rate=decay_rate, level_row_index=level_row_index, level_weight_table=level_weight_table)


epsilon = 1e-06
highest = lax.Precision.HIGHEST

def rounded(values):
    return lax.optimization_barrier(values.astype(jnp.bfloat16)).astype(jnp.float32)

def head_mix(inputs):
    queries, key_rows, value_rows, rates, level_mix = inputs
    block_count = SEQUENCE_SPAN // BLOCK
    queries = queries.astype(jnp.float32).reshape(block_count, BLOCK, DH)
    key_rows = key_rows.astype(jnp.float32).reshape(block_count, BLOCK, DH)
    value_rows = value_rows.astype(jnp.float32).reshape(block_count, BLOCK, DH)
    decay_log = jnp.cumsum(-rates.reshape(block_count, BLOCK), axis=1)
    block_total = decay_log[:, -1]
    level_mix = level_mix.reshape(block_count, BLOCK, LEVEL_COUNT)
    positions = jnp.arange(BLOCK, dtype=jnp.int32)
    causal = positions[:, None] >= positions[None, :]
    gap_log = jnp.where(causal, decay_log[:, :, None] - decay_log[:, None, :], jnp.float32(0.0))
    scores = jnp.einsum('cid,cjd->cij', queries, key_rows)
    weights = rounded(jnp.where(causal, scores * jnp.exp(gap_log), jnp.float32(0.0)) * level_mix[:, :, 0][:, :, None])
    within = jnp.einsum('cij,cjd->cid', weights, value_rows)
    decayed_keys = rounded(key_rows * jnp.exp(block_total[:, None] - decay_log)[:, :, None])
    group_states = jnp.einsum('cjd,cje->cde', decayed_keys, value_rows)
    decayed_queries = queries * jnp.exp(decay_log)[:, :, None]
    block_index = jnp.arange(block_count, dtype=jnp.int32)
    group_totals = block_total
    offsets = jnp.zeros_like(block_total)
    spanned = jnp.zeros_like(within)
    for level in range(1, LEVEL_COUNT):
        group_size = 2 ** (level - 1)
        upper_half = (block_index // group_size % 2).astype(jnp.float32)
        lower_group = jnp.maximum(block_index // group_size - 1, 0).astype(jnp.int32)
        chosen = group_states[lower_group]
        factor = upper_half * jnp.exp(offsets)
        contrib = jnp.einsum('cid,cde->cie', decayed_queries * factor[:, None, None], chosen, precision=highest)
        spanned = spanned + contrib * level_mix[:, :, level][:, :, None]
        offsets = offsets + upper_half * group_totals[lower_group]
        group_states = jnp.exp(group_totals[1::2])[:, None, None] * group_states[0::2] + group_states[1::2]
        group_totals = group_totals[0::2] + group_totals[1::2]
    mixed = within + spanned
    mixed = mixed * lax.rsqrt(lax.optimization_barrier(jnp.mean(mixed * mixed, axis=-1, keepdims=True)) + epsilon)
    return mixed.reshape(SEQUENCE_SPAN, DH).astype(jnp.bfloat16)

def reference(tokens, w_query, w_key, w_value, w_out, decay_rate, level_row_index, level_weight_table):

    def project(weight_cols):
        result = jnp.dot(tokens, weight_cols, preferred_element_type=jnp.float32).astype(jnp.bfloat16)
        return result.reshape(SEQUENCE_SPAN, ATTENDER_NUMBER, DH).transpose(1, 0, 2)
    level_mix = level_weight_table[level_row_index].transpose(1, 0, 2)
    normed = lax.map(head_mix, (project(w_query), project(w_key), project(w_value), decay_rate.T, level_mix))
    normed = normed.transpose(1, 0, 2).reshape(SEQUENCE_SPAN, ATTENDER_NUMBER * DH)
    group_width = HEAD_DEV * DH
    summed = jnp.zeros((SEQUENCE_SPAN, D), jnp.float32)
    for group_index in range(ATTENDER_NUMBER // HEAD_DEV):
        lower_edge = group_index * group_width
        upper_edge = lower_edge + group_width
        partial_value = jnp.dot(normed[:, lower_edge:upper_edge], w_out[lower_edge:upper_edge], preferred_element_type=jnp.float32)
        summed = summed + rounded(partial_value)
    return summed.astype(jnp.bfloat16)
```

```python
import functools

import jax
import jax.numpy as jnp
from jax import lax
from jax.experimental import pallas as pl
from jax.experimental.pallas import tpu as pltpu
from jax.sharding import PartitionSpec as P

F32, BF16 = jnp.float32, jnp.bfloat16
MESH = pl.DeviceIdType.MESH
EPSILON = 1e-06
DH = 128
HEADS = 2
CHUNK = 256
CHUNKS = 8
HALF = CHUNKS // 2
LOCAL = 3
CTX_Z, CTX_Y = 3, 2
CROSS = CTX_Z + CTX_Y
FIRST_LOCAL, FIRST_CROSS = 3, 6
ROWS = 16
CUM, KDEC = 11, 12
MSG = DH + 16


def dot(a, b, dims=((1,), (0,))):
    return lax.dot_general(a, b, (dims, ((), ())), preferred_element_type=F32)


def split(x, terms):
    parts = []
    for _ in range(terms):
        part = x.astype(BF16)
        parts.append(part)
        x = x - part.astype(F32)
    return parts


def mirror(index, bits):
    size = 2**bits
    low = lax.rem(index, size)
    return index - low + (size - 1 - low)


def kernel(
    tokens, w_query, w_key, w_value, w_out, rates, row_index, table,
    out,
    tok, wkv, wq, kv, states, local_states, local_out, cross_lhs, cross_states,
    table_rows, rate_rows, cum_rows, cols, send_state, recv_state,
    gathered, other, weights, spare, staged,
    tok_sem, w_sem, wl_sem, ws_send, ws_recv, wx_send, wx_recv,
    st_send, st_recv, g_send, g_recv,
):
    pos = lax.axis_index("ctx")
    me = lax.axis_index("head")
    x = lax.div(me, 2)
    core = lax.rem(me, 2)
    pair = x + 1 - 2 * lax.rem(x, 2)
    across = 3 - x
    far = lax.rem(x + 2, 4)
    z = lax.rem(pos, 2**CTX_Z)
    y = lax.div(pos, 2**CTX_Z)
    sibling_id = (pos, 2 * x + 1 - core)
    pair_id = (pos, 2 * pair + core)
    across_id = (pos, 2 * across + core)
    far_id = (pos, 2 * far + core)
    ctx_ids = [(y * 2**CTX_Z + mirror(z, b + 1), me) for b in range(CTX_Z)]
    ctx_ids += [(mirror(y, b + 1) * 2**CTX_Z + z, me) for b in range(CTX_Y)]
    partners = [sibling_id, pair_id, across_id, far_id] + ctx_ids

    barrier = pltpu.get_barrier_semaphore()
    for partner in partners:
        pl.semaphore_signal(barrier, inc=1, device_id=partner, device_id_type=MESH)

    def weight_copy(source, head, part):
        return pltpu.make_async_copy(
            source.at[:, pl.ds(head * DH, DH)],
            wkv.at[head, :, pl.ds(part * DH, DH)],
            w_sem.at[head * 2 + part],
        )

    def token_copy(u):
        return pltpu.make_async_copy(
            tokens.at[pl.ds(pl.multiple_of(u * CHUNK, CHUNK), CHUNK), :], tok.at[u], tok_sem.at[u]
        )

    query_copy = pltpu.make_async_copy(w_query, wq, w_sem.at[4])
    weight_copy(w_key, 0, 0).start()
    weight_copy(w_value, 0, 1).start()
    for u in range(CHUNKS):
        token_copy(u).start()
        if u == 2:
            weight_copy(w_key, 1, 0).start()
            weight_copy(w_value, 1, 1).start()
    query_copy.start()

    homes = [(weights, 0, 0, x), (weights, 0, 1, across), (spare, None, 0, far), (spare, None, 1, pair)]

    def piece(buffer, slot, a, k):
        view = buffer.at[slot, a] if slot is not None else buffer.at[a]
        return view.at[pl.ds(k * 256, 256), :]

    own_pieces, sibling_pieces = [], []
    for i, (buffer, slot, a, chip) in enumerate(homes):
        columns = pl.ds(pl.multiple_of((2 * chip + core) * 256, 256), 256)
        own_pieces.append(
            pltpu.make_async_copy(w_out.at[:, columns], piece(buffer, slot, a, 0), wl_sem.at[i])
        )
        columns = pl.ds(pl.multiple_of((2 * chip + 1 - core) * 256, 256), 256)
        sibling_pieces.append(
            pltpu.make_async_remote_copy(
                src_ref=w_out.at[:, columns],
                dst_ref=piece(buffer, slot, a, 1),
                send_sem=ws_send.at[i],
                recv_sem=ws_recv.at[i],
                device_id=sibling_id,
                device_id_type=MESH,
            )
        )
        own_pieces[-1].start()

    def weight_send(i, source, slot, target):
        return pltpu.make_async_remote_copy(
            src_ref=source, dst_ref=weights.at[slot], send_sem=wx_send.at[i],
            recv_sem=wx_recv.at[i], device_id=target, device_id_type=MESH,
        )

    weight_sends = [
        weight_send(0, weights.at[0], 2, across_id),
        weight_send(1, spare, 1, pair_id),
        weight_send(2, spare, 3, far_id),
    ]

    for u in range(CHUNKS):
        rate_rows[HEADS * u : HEADS * (u + 1), :] = rates[:, u * CHUNK : (u + 1) * CHUNK]
    before = lax.broadcasted_iota(jnp.int32, (CHUNK, CHUNK), 0)
    after = lax.broadcasted_iota(jnp.int32, (CHUNK, CHUNK), 1)
    upper = (before <= after).astype(BF16)
    cum = sum(dot(part, upper) for part in split(-rate_rows[...], 3))
    cum_rows[...] = cum
    last = cum[:, CHUNK - 1 :]
    key_decay = jnp.exp(last - cum)
    totals = [[last[HEADS * u + h : HEADS * u + h + 1, :] for u in range(CHUNKS)] for h in range(HEADS)]

    table_rows[...] = jnp.zeros_like(table_rows)
    levels = table.shape[0]
    for h in range(HEADS):
        table_rows[h * ROWS : h * ROWS + levels, :] = table[:, h, :]
    slots = table.shape[2]
    parts = split(table_rows[...], 3)
    level = lax.broadcasted_iota(jnp.int32, (ROWS, 1), 0)
    for u in range(CHUNKS):
        span = slice(u * CHUNK, (u + 1) * CHUNK)
        chosen = lax.broadcasted_iota(jnp.int32, (slots, CHUNK), 0) == row_index[:, span]
        chosen = jnp.where(chosen, 1.0, 0.0).astype(BF16)
        mix = sum(dot(part, chosen) for part in parts)
        rows = []
        for h in range(HEADS):
            none = jnp.zeros((1, 1), F32)
            offsets = [
                none,
                totals[h][u - 1] if u % 2 else none,
                sum(totals[h][4:u], none),
                sum(totals[h][:u], none),
            ]
            offset = jnp.where(level == 4, offsets[1], offsets[0])
            offset = jnp.where(level == 5, offsets[2], offset)
            offset = jnp.where(level >= FIRST_CROSS, offsets[3], offset)
            here = HEADS * u + h
            cum_row = cum[here : here + 1, :]
            factor = jnp.exp(jnp.where(level >= FIRST_LOCAL, cum_row + offset, 0.0))
            for bit in range(LOCAL):
                if not (u >> bit) & 1:
                    factor = jnp.where(level == FIRST_LOCAL + bit, 0.0, factor)
            table_of_rows = mix[h * ROWS : (h + 1) * ROWS, :] * factor
            table_of_rows = jnp.where(level == CUM, cum_row, table_of_rows)
            table_of_rows = jnp.where(level == KDEC, key_decay[here : here + 1, :], table_of_rows)
            rows.append(table_of_rows)
        cols[u, :, 0 : HEADS * ROWS] = jnp.concatenate(rows, axis=0).T

    pl.semaphore_wait(barrier, len(partners))
    for copy in sibling_pieces:
        copy.start()

    def key_value(h, u):
        result = dot(tok[u], wkv[h]).astype(BF16)
        kv[h, u] = result
        decay = cols[u, :, pl.ds(h * ROWS + KDEC, 1)]
        decayed = (result[:, :DH].astype(F32) * decay).astype(BF16)
        states[h, u] = dot(decayed, result[:, DH:], ((0,), (0,)))

    def merge(first, second):
        return jnp.exp(second[1]) * first[0] + second[0], first[1] + second[1]

    running = [None] * HEADS
    passed = [jnp.zeros((1, 1), F32) for _ in range(HEADS)]

    def state_copy(h, b):
        return pltpu.make_async_remote_copy(
            src_ref=send_state.at[h, b], dst_ref=recv_state.at[h, b], send_sem=st_send.at[h, b],
            recv_sem=st_recv.at[h, b], device_id=ctx_ids[b], device_id_type=MESH,
        )

    def send(h, b):
        state, total = running[h]
        send_state[h, b, 0:DH, :] = state.astype(BF16)
        row = lax.broadcasted_iota(jnp.int32, (16, DH), 0)
        tail = jnp.zeros((16, DH), F32)
        for i, part in enumerate(split(total, 3)):
            tail = jnp.where(row == i, part.astype(F32), tail)
        send_state[h, b, DH:MSG, :] = tail.astype(BF16)
        state_copy(h, b).start()

    def receive(h, b):
        state_copy(h, b).wait_recv()
        there = recv_state[h, b, 0:DH, :].astype(F32)
        tail = recv_state[h, b, DH:MSG, :].astype(F32)
        there_total = tail[0:1, 0:1] + tail[1:2, 0:1] + tail[2:3, 0:1]
        is_upper = lax.rem(lax.div(pos, 2**b), 2) == 1
        cross = jnp.where(is_upper, jnp.exp(passed[h]) * there, 0.0)
        cross_states[h, b * DH : (b + 1) * DH, :] = cross.astype(BF16)
        state, total = running[h]
        passed[h] = passed[h] + jnp.where(is_upper, there_total, 0.0)
        low = jnp.where(is_upper, there, state)
        high = jnp.where(is_upper, state, there)
        high_total = jnp.where(is_upper, total, there_total)
        running[h] = (jnp.exp(high_total) * low + high, total + there_total)
        if b + 1 < CROSS:
            send(h, b + 1)

    def own_state(h):
        single = [(states[h, u], totals[h][u]) for u in range(CHUNKS)]
        pairs = [merge(single[2 * i], single[2 * i + 1]) for i in range(4)]
        quads = [merge(pairs[2 * i], pairs[2 * i + 1]) for i in range(2)]
        running[h] = merge(quads[0], quads[1])
        send(h, 0)
        zero = jnp.zeros((DH, DH), BF16)
        for u in range(CHUNKS):
            lower = [
                single[u - 1][0].astype(BF16) if u & 1 else zero,
                pairs[u // 2 - 1][0].astype(BF16) if u & 2 else zero,
                quads[0][0].astype(BF16) if u & 4 else zero,
            ]
            for i, state in enumerate(lower):
                local_states[h, u, i * DH : (i + 1) * DH, :] = state

    weight_copy(w_key, 0, 0).wait()
    weight_copy(w_value, 0, 1).wait()

    def first_head(u, carry):
        token_copy(u).wait()
        key_value(0, u)
        return carry

    lax.fori_loop(0, CHUNKS, first_head, 0)
    own_state(0)

    for copy in own_pieces:
        copy.wait()
    for copy in sibling_pieces:
        copy.wait_recv()
    for copy in weight_sends:
        copy.start()

    weight_copy(w_key, 1, 0).wait()
    weight_copy(w_value, 1, 1).wait()

    def second_head(u, carry):
        key_value(1, u)
        return carry

    lax.fori_loop(0, CHUNKS, second_head, 0)
    own_state(1)
    receive(0, 0)
    query_copy.wait()

    def local_part(u, carry):
        queries = dot(tok[u], wq[...]).astype(BF16)
        token = lax.broadcasted_iota(jnp.int32, (CHUNK, CHUNK), 0)
        source = lax.broadcasted_iota(jnp.int32, (CHUNK, CHUNK), 1)
        causal = token >= source
        same_block = lax.div(token, 64) == lax.div(source, 64)
        same_pair = lax.div(token, 128) == lax.div(source, 128)
        for h in range(HEADS):
            column = lambda row: cols[u, :, pl.ds(h * ROWS + row, 1)]
            query = queries[:, h * DH : (h + 1) * DH]
            key, value = kv[h, u, :, 0:DH], kv[h, u, :, DH : 2 * DH]
            gap = column(CUM) - cum_rows[pl.ds(HEADS * u + h, 1), :]
            decay = jnp.exp(jnp.where(causal, gap, -1e30))
            mix = jnp.where(same_block, column(0), jnp.where(same_pair, column(1), column(2)))
            scores = dot(query, key, ((1,), (1,)))
            result = dot((scores * decay * mix).astype(BF16), value)
            query = query.astype(F32)
            lhs = [(query * column(FIRST_LOCAL + i)).astype(BF16) for i in range(LOCAL)]
            result += dot(jnp.concatenate(lhs, axis=1), local_states[h, u])
            local_out[u, :, h * DH : (h + 1) * DH] = result
            for i in range(CROSS):
                cross_lhs[u, h, :, i * DH : (i + 1) * DH] = (
                    query * column(FIRST_CROSS + i)
                ).astype(BF16)
        return carry

    lax.fori_loop(0, 3, local_part, 0)
    receive(1, 0)
    receive(0, 1)
    lax.fori_loop(3, 6, local_part, 0)
    receive(1, 1)
    receive(0, 2)
    lax.fori_loop(6, CHUNKS, local_part, 0)
    receive(1, 2)
    receive(0, 3)
    receive(1, 3)
    receive(0, 4)
    receive(1, 4)

    mine = lax.div(x, 2)

    def moved(kind, j, source, target_slot, target):
        return pltpu.make_async_remote_copy(
            src_ref=source, dst_ref=slot(j, target_slot), send_sem=g_send.at[kind, j],
            recv_sem=g_recv.at[kind, j], device_id=target, device_id_type=MESH,
        )

    def slot(j, number):
        return gathered.at[j, :, pl.ds(number * 256, 256)]

    def own_to_sibling(j):
        return moved(0, j, slot(j, 0), 1, sibling_id)

    def own_to_pair(j):
        return moved(1, j, slot(j, 0), 2, pair_id)

    def pair_to_sibling(j):
        return moved(2, j, slot(j, 2), 3, sibling_id)

    def other_to_across(j):
        return moved(3, j, other.at[j], 4, across_id)

    def across_to_sibling(j):
        return moved(4, j, slot(j, 4), 5, sibling_id)

    def across_to_pair(j):
        return moved(5, j, slot(j, 4), 6, pair_id)

    def far_to_sibling(j):
        return moved(6, j, slot(j, 6), 7, sibling_id)

    def mine_rows(j):
        return pl.ds(pl.multiple_of((mine * HALF + j) * CHUNK, CHUNK), CHUNK)

    def result_to_across(j):
        return pltpu.make_async_remote_copy(
            src_ref=staged.at[j], dst_ref=out.at[mine_rows(j), :], send_sem=g_send.at[7, j],
            recv_sem=g_recv.at[7, j], device_id=across_id, device_id_type=MESH,
        )

    def normed(u):
        heads = []
        for h in range(HEADS):
            value = local_out[u, :, h * DH : (h + 1) * DH] + dot(cross_lhs[u, h], cross_states[h])
            square = jnp.mean(value * value, axis=1, keepdims=True)
            heads.append((value * lax.rsqrt(square + EPSILON)).astype(BF16))
        return jnp.concatenate(heads, axis=1)

    def finish(j, carry):
        other[j] = normed((1 - mine) * HALF + j)
        other_to_across(j).start()
        gathered[j, :, 0:256] = normed(mine * HALF + j)
        own_to_pair(j).start()
        own_to_sibling(j).start()
        return carry

    lax.fori_loop(0, HALF, finish, 0)

    def forward(j, carry):
        other_to_across(j).wait_recv()
        across_to_pair(j).start()
        across_to_sibling(j).start()
        own_to_pair(j).wait_recv()
        pair_to_sibling(j).start()
        return carry

    lax.fori_loop(0, HALF, forward, 0)
    for copy in weight_sends:
        copy.wait_recv()

    for_own, for_across = (0, 1, 1, 0), (1, 0, 0, 1)

    def project(j, carry):
        across_to_pair(j).wait_recv()
        far_to_sibling(j).start()
        own_to_sibling(j).wait_recv()
        pair_to_sibling(j).wait_recv()
        across_to_sibling(j).wait_recv()

        def product(a, r):
            return dot(gathered[j, :, r * 512 : (r + 1) * 512], weights[r, a[r]])

        to_across = product(for_across, 0) + product(for_across, 1) + product(for_across, 2)
        to_own = product(for_own, 0) + product(for_own, 1) + product(for_own, 2)
        far_to_sibling(j).wait_recv()
        staged[j] = (to_across + product(for_across, 3)).astype(BF16)
        result_to_across(j).start()
        out[mine_rows(j), :] = (to_own + product(for_own, 3)).astype(BF16)
        return carry

    lax.fori_loop(0, HALF, project, 0)

    def drain(j, carry):
        for copy in (
            own_to_sibling, own_to_pair, pair_to_sibling, other_to_across,
            across_to_sibling, across_to_pair, far_to_sibling,
        ):
            copy(j).wait_send()
        result_to_across(j).wait()
        return carry

    lax.fori_loop(0, HALF, drain, 0)
    for copy in sibling_pieces + weight_sends:
        copy.wait_send()
    for h in range(HEADS):
        for b in range(CROSS):
            state_copy(h, b).wait_send()


def shards(tokens, w_query, w_key, w_value, w_out, decay_rate, level_row_index, level_weight_table):
    rows, depth = tokens.shape
    width = w_query.shape[1]
    vmem = functools.partial(pltpu.VMEM)
    dma = pltpu.SemaphoreType.DMA
    hbm, on_chip = pl.BlockSpec(memory_space=pl.ANY), pl.BlockSpec(memory_space=pltpu.VMEM)
    call = pl.pallas_call(
        kernel,
        out_shape=jax.ShapeDtypeStruct((rows, width), BF16),
        in_specs=[hbm] * 5 + [on_chip] * 3,
        out_specs=on_chip,
        scratch_shapes=[
            vmem((CHUNKS, CHUNK, depth), BF16),
            vmem((HEADS, depth, 2 * DH), BF16),
            vmem((depth, width), BF16),
            vmem((HEADS, CHUNKS, CHUNK, 2 * DH), BF16),
            vmem((HEADS, CHUNKS, DH, DH), F32),
            vmem((HEADS, CHUNKS, LOCAL * DH, DH), BF16),
            vmem((CHUNKS, CHUNK, width), F32),
            vmem((CHUNKS, HEADS, CHUNK, CROSS * DH), BF16),
            vmem((HEADS, CROSS * DH, DH), BF16),
            vmem((HEADS * ROWS, level_weight_table.shape[0]), F32),
            vmem((HEADS * CHUNKS, CHUNK), F32),
            vmem((HEADS * CHUNKS, CHUNK), F32),
            vmem((CHUNKS, CHUNK, 128), F32),
            vmem((HEADS, CROSS, MSG, DH), BF16),
            vmem((HEADS, CROSS, MSG, DH), BF16),
            vmem((HALF, CHUNK, 8 * width), BF16),
            vmem((HALF, CHUNK, width), BF16),
            vmem((4, 2, 2 * width, width), BF16),
            vmem((2, 2 * width, width), BF16),
            vmem((HALF, CHUNK, width), BF16),
            dma((CHUNKS,)), dma((5,)), dma((4,)), dma((4,)), dma((4,)), dma((3,)), dma((3,)),
            dma((HEADS, CROSS)), dma((HEADS, CROSS)), dma((8, HALF)), dma((8, HALF)),
        ],
        compiler_params=pltpu.CompilerParams(
            collective_id=0, has_side_effects=True, vmem_limit_bytes=56 * 2**20
        ),
    )
    return call(
        tokens, w_query, w_key, w_value, w_out, decay_rate.T, level_row_index.reshape(1, rows),
        level_weight_table.transpose(2, 1, 0),
    )


def solution(mesh):
    placed = (
        P("ctx", None),
        P(None, "head"),
        P(None, "head"),
        P(None, "head"),
        P("head", None),
        P("ctx", "head"),
        P("ctx"),
        P(None, "head", None),
    )
    return jax.shard_map(
        shards, mesh=mesh, in_specs=placed, out_specs=P("ctx", "head"), check_vma=False
    )
```

```python
import functools

import jax
import jax.numpy as jnp
from jax import lax
from jax.experimental import pallas as pl
from jax.experimental.pallas import tpu as pltpu
from jax.sharding import PartitionSpec as P

F32, BF16 = jnp.float32, jnp.bfloat16
MESH = pl.DeviceIdType.MESH
EPSILON = 1e-06
DH = 128
HEADS = 2
CHUNK = 256
CHUNKS = 8
HALF = CHUNKS // 2
LOCAL = 3
PLACES_Z, PLACES_Y = 8, 4
CTX_Z, CTX_Y = 3, 2
CROSS = CTX_Z + CTX_Y
TALL = 2
FIRST_LOCAL, FIRST_CROSS = 3, 6
ROWS = 16
CUM = 11
MSG = DH + 16
NEVER = -1e30


def dot(a, b, dims=((1,), (0,))):
    return lax.dot_general(a, b, (dims, ((), ())), preferred_element_type=F32)


def split(x, terms):
    parts = []
    for _ in range(terms):
        part = x.astype(BF16)
        parts.append(part)
        x = x - part.astype(F32)
    return parts


def kernel(
    tokens, w_query, w_key, w_value, w_out, rates, row_index, table,
    out,
    tok, wkv, wq, kv, local_states, local_out, cross_lhs, cross_states,
    table_rows, table_parts, rate_rows, cum_rows, offset_rows, send_state, recv_state,
    gathered, other, weights, spare, staged,
    tok_sem, w_sem, wl_sem, ws_send, ws_recv, wx_send, wx_recv,
    st_send, st_recv, g_send, g_recv, out_send, out_recv,
):
    pos = lax.axis_index("ctx")
    me = lax.axis_index("head")
    x = lax.div(me, 2)
    core = lax.rem(me, 2)
    pair = x + 1 - 2 * lax.rem(x, 2)
    across = 3 - x
    far = lax.rem(x + 2, 4)
    z = lax.rem(pos, PLACES_Z)
    y = lax.div(pos, PLACES_Z)
    sibling_id = (pos, 2 * x + 1 - core)
    pair_id = (pos, 2 * pair + core)
    across_id = (pos, 2 * across + core)
    far_id = (pos, 2 * far + core)
    z_bits = [lax.rem(lax.div(z, 2**b), 2) for b in range(CTX_Z)]
    flips = [2**b * (1 - 2 * z_bits[b]) for b in range(CTX_Z)]
    state_ids = [(pos + shift, me) for shift in (flips[0], flips[1], flips[1] + flips[2])]
    state_ids += [(lax.rem(y + d, PLACES_Y) * PLACES_Z + z, me) for d in range(1, PLACES_Y)]
    partners = [sibling_id, pair_id, across_id, far_id] + state_ids

    barrier = pltpu.get_barrier_semaphore()
    for partner in partners:
        pl.semaphore_signal(barrier, inc=1, device_id=partner, device_id_type=MESH)

    def weight_copy(source, head, part):
        return pltpu.make_async_copy(
            source.at[:, pl.ds(head * DH, DH)],
            wkv.at[head, :, pl.ds(part * DH, DH)],
            w_sem.at[head * 2 + part],
        )

    def token_rows(u, count):
        return pl.ds(pl.multiple_of(u * CHUNK, CHUNK), count * CHUNK)

    def token_copy(u):
        return pltpu.make_async_copy(
            tokens.at[token_rows(u, 1), :], tok.at[token_rows(u, 1), :], tok_sem.at[u]
        )

    query_copy = pltpu.make_async_copy(w_query, wq, w_sem.at[4])
    weight_copy(w_key, 0, 0).start()
    weight_copy(w_value, 0, 1).start()
    for u in range(CHUNKS):
        token_copy(u).start()
    weight_copy(w_key, 1, 0).start()
    weight_copy(w_value, 1, 1).start()
    query_copy.start()

    homes = [(weights, 0, 0, x), (weights, 0, 1, across), (spare, None, 0, far), (spare, None, 1, pair)]

    def piece(buffer, slot, a, k):
        view = buffer.at[slot, a] if slot is not None else buffer.at[a]
        return view.at[:, k]

    own_pieces, sibling_pieces = [], []
    for i, (buffer, slot, a, chip) in enumerate(homes):
        columns = pl.ds(pl.multiple_of((2 * chip + core) * 256, 256), 256)
        own_pieces.append(
            pltpu.make_async_copy(w_out.at[:, :, columns], piece(buffer, slot, a, 0), wl_sem.at[i])
        )
        columns = pl.ds(pl.multiple_of((2 * chip + 1 - core) * 256, 256), 256)
        sibling_pieces.append(
            pltpu.make_async_remote_copy(
                src_ref=w_out.at[:, :, columns],
                dst_ref=piece(buffer, slot, a, 1),
                send_sem=ws_send.at[i],
                recv_sem=ws_recv.at[i],
                device_id=sibling_id,
                device_id_type=MESH,
            )
        )

    def weight_send(i, source, slot, target):
        return pltpu.make_async_remote_copy(
            src_ref=source, dst_ref=weights.at[slot], send_sem=wx_send.at[i],
            recv_sem=wx_recv.at[i], device_id=target, device_id_type=MESH,
        )

    weight_sends = [
        weight_send(0, weights.at[0], 2, across_id),
        weight_send(1, spare, 1, pair_id),
        weight_send(2, spare, 3, far_id),
    ]

    for u in range(CHUNKS):
        rate_rows[HEADS * u : HEADS * (u + 1), :] = rates[:, u * CHUNK : (u + 1) * CHUNK]
    before = lax.broadcasted_iota(jnp.int32, (CHUNK, CHUNK), 0)
    after = lax.broadcasted_iota(jnp.int32, (CHUNK, CHUNK), 1)
    upper = (before <= after).astype(BF16)
    cum = sum(dot(part, upper) for part in split(-rate_rows[...], 3))
    cum_rows[...] = cum
    last = cum[:, CHUNK - 1 :]
    key_decay = jnp.exp(last - cum).T
    totals = [[last[HEADS * u + h : HEADS * u + h + 1, :] for u in range(CHUNKS)] for h in range(HEADS)]

    table_rows[...] = jnp.zeros_like(table_rows)
    levels = table.shape[0]
    for h in range(HEADS):
        table_rows[h * ROWS : h * ROWS + levels, :] = table[:, h, :]
    for i, part in enumerate(split(table_rows[...], 3)):
        table_parts[i] = part
    level = lax.broadcasted_iota(jnp.int32, (ROWS, 128), 0)
    none = jnp.zeros((1, 1), F32)
    for u in range(CHUNKS):
        for h in range(HEADS):
            offset = jnp.where(level >= FIRST_CROSS, sum(totals[h][:u], none), none)
            ends = [none, totals[h][u - 1] if u % 2 else none, sum(totals[h][4:u], none)]
            for bit in range(LOCAL):
                end = ends[bit] if (u >> bit) & 1 else NEVER
                offset = jnp.where(level == FIRST_LOCAL + bit, end, offset)
            offset_rows[HEADS * u + h] = offset

    def key_value(h, i):
        result = dot(tok[token_rows(i * TALL, TALL), :], wkv[h]).astype(BF16)
        for part in range(TALL):
            kv[h, i * TALL + part] = result[part * CHUNK : (part + 1) * CHUNK]

    def chunk_state(h, u):
        decay = key_decay[:, HEADS * u + h : HEADS * u + h + 1]
        decayed = (kv[h, u, :, :DH].astype(F32) * decay).astype(BF16)
        return dot(decayed, kv[h, u, :, DH:], ((0,), (0,)))

    def merge(first, second):
        return jnp.exp(second[1]) * first[0] + second[0], first[1] + second[1]

    running = [None] * HEADS
    passed = [jnp.zeros((1, 1), F32) for _ in range(HEADS)]

    def state_copy(h, b):
        return pltpu.make_async_remote_copy(
            src_ref=send_state.at[h, min(b, CTX_Z)], dst_ref=recv_state.at[h, b], send_sem=st_send.at[h, b],
            recv_sem=st_recv.at[h, b], device_id=state_ids[b], device_id_type=MESH,
        )

    def send(h, b):
        state, total = running[h]
        send_state[h, b, 0:DH, :] = state.astype(BF16)
        row = lax.broadcasted_iota(jnp.int32, (16, DH), 0)
        tail = jnp.zeros((16, DH), F32)
        for i, part in enumerate(split(total, 3)):
            tail = jnp.where(row == i, part.astype(F32), tail)
        send_state[h, b, DH:MSG, :] = tail.astype(BF16)
        for step in [b] if b < CTX_Z else range(CTX_Z, CTX_Z + PLACES_Y - 1):
            state_copy(h, step).start()

    def arrived(h, b):
        state_copy(h, b).wait_recv()
        tail = recv_state[h, b, DH:MSG, :].astype(F32)
        return recv_state[h, b, 0:DH, :].astype(F32), tail[0:1, 0:1] + tail[1:2, 0:1] + tail[2:3, 0:1]

    def keep_cross(h, b, state):
        cross_states[h, b * DH : (b + 1) * DH, :] = state.astype(BF16)

    def receive_z(h, b):
        there, there_total = arrived(h, b)
        is_upper = z_bits[b] == 1
        state, total = running[h]
        low = jnp.where(is_upper, there, state)
        high = jnp.where(is_upper, state, there)
        high_total = jnp.where(is_upper, total, there_total)
        running[h] = (jnp.exp(high_total) * low + high, total + there_total)
        send(h, b + 1)
        keep_cross(h, b, jnp.where(is_upper, jnp.exp(passed[h]) * there, 0.0))
        passed[h] = passed[h] + jnp.where(is_upper, there_total, 0.0)

    def receive_y(h):
        behind = [arrived(h, CTX_Z + d) for d in range(PLACES_Y - 1)]
        is_odd, is_upper = lax.rem(y, 2) == 1, lax.div(y, 2) == 1
        (one, one_total), (two, two_total), (three, _) = behind
        keep_cross(h, CTX_Z, jnp.where(is_odd, jnp.exp(passed[h]) * one, 0.0))
        first, second = jnp.where(is_odd, three, two), jnp.where(is_odd, two, one)
        second_total = jnp.where(is_odd, two_total, one_total)
        ahead = passed[h] + jnp.where(is_odd, one_total, 0.0)
        both = jnp.exp(ahead) * (jnp.exp(second_total) * first + second)
        keep_cross(h, CTX_Z + 1, jnp.where(is_upper, both, 0.0))

    def own_state(h):
        single = [(chunk_state(h, u), totals[h][u]) for u in range(CHUNKS)]
        pairs = [merge(single[2 * i], single[2 * i + 1]) for i in range(4)]
        quads = [merge(pairs[2 * i], pairs[2 * i + 1]) for i in range(2)]
        running[h] = merge(quads[0], quads[1])
        send(h, 0)
        zero = jnp.zeros((DH, DH), BF16)
        for u in range(CHUNKS):
            lower = [
                single[u - 1][0].astype(BF16) if u & 1 else zero,
                pairs[u // 2 - 1][0].astype(BF16) if u & 2 else zero,
                quads[0][0].astype(BF16) if u & 4 else zero,
            ]
            for i, state in enumerate(lower):
                local_states[h, u, i * DH : (i + 1) * DH, :] = state

    weight_copy(w_key, 0, 0).wait()
    weight_copy(w_value, 0, 1).wait()

    def first_head(i, carry):
        for part in range(TALL):
            token_copy(i * TALL + part).wait()
        key_value(0, i)
        return carry

    def second_head(i, carry):
        key_value(1, i)
        return carry

    for copy in own_pieces:
        copy.start()
    lax.fori_loop(0, 1, first_head, 0)
    pl.semaphore_wait(barrier, len(partners))
    for copy in sibling_pieces:
        copy.start()
    lax.fori_loop(1, 3, first_head, 0)
    for copy in own_pieces:
        copy.wait()
    for copy in sibling_pieces:
        copy.wait_recv()
    for copy in weight_sends:
        copy.start()
    lax.fori_loop(3, CHUNKS // TALL, first_head, 0)
    own_state(0)

    weight_copy(w_key, 1, 0).wait()
    weight_copy(w_value, 1, 1).wait()
    lax.fori_loop(0, CHUNKS // TALL, second_head, 0)
    receive_z(0, 0)
    own_state(1)
    query_copy.wait()

    def local_part(u, carry):
        queries = dot(tok[token_rows(u, 1), :], wq[...]).astype(BF16)
        slots = table.shape[2]
        chosen = lax.broadcasted_iota(jnp.int32, (slots, CHUNK), 0) == row_index[:, token_rows(u, 1)]
        chosen = jnp.where(chosen, 1.0, 0.0).astype(BF16)
        level_mix = sum(dot(table_parts[i], chosen) for i in range(3))
        row = lax.broadcasted_iota(jnp.int32, (ROWS, CHUNK), 0)
        rows = []
        for h in range(HEADS):
            cum_row = cum_rows[pl.ds(HEADS * u + h, 1), :]
            decay = cum_row + offset_rows[HEADS * u + h][:, 0:1]
            factor = jnp.exp(jnp.where(row >= FIRST_LOCAL, decay, 0.0))
            scaled = level_mix[h * ROWS : (h + 1) * ROWS, :] * factor
            rows.append(jnp.where(row == CUM, cum_row, scaled))
        cols = jnp.concatenate(rows, axis=0).T
        token = lax.broadcasted_iota(jnp.int32, (CHUNK, CHUNK), 0)
        source = lax.broadcasted_iota(jnp.int32, (CHUNK, CHUNK), 1)
        causal = token >= source
        same_block = lax.div(token, 64) == lax.div(source, 64)
        same_pair = lax.div(token, 128) == lax.div(source, 128)
        for h in range(HEADS):
            column = lambda row: cols[:, h * ROWS + row : h * ROWS + row + 1]
            query = queries[:, h * DH : (h + 1) * DH]
            key, value = kv[h, u, :, 0:DH], kv[h, u, :, DH : 2 * DH]
            gap = column(CUM) - cum_rows[pl.ds(HEADS * u + h, 1), :]
            decay = jnp.exp(jnp.where(causal, gap, NEVER))
            mix = jnp.where(same_block, column(0), jnp.where(same_pair, column(1), column(2)))
            scores = dot(query, key, ((1,), (1,)))
            result = dot((scores * decay * mix).astype(BF16), value)
            query = query.astype(F32)
            lhs = [(query * column(FIRST_LOCAL + i)).astype(BF16) for i in range(LOCAL)]
            result += dot(jnp.concatenate(lhs, axis=1), local_states[h, u])
            local_out[u, :, h * DH : (h + 1) * DH] = result
            for i in range(CROSS):
                cross_lhs[u, h, :, i * DH : (i + 1) * DH] = (
                    query * column(FIRST_CROSS + i)
                ).astype(BF16)
        return carry

    lax.fori_loop(0, 2, local_part, 0)
    receive_z(1, 0)
    receive_z(0, 1)
    lax.fori_loop(2, 5, local_part, 0)
    receive_z(1, 1)
    receive_z(0, 2)
    lax.fori_loop(5, CHUNKS, local_part, 0)
    receive_z(1, 2)

    mine = lax.div(x, 2)

    def slot(j, h, number):
        return gathered.at[j, h, :, pl.ds(number * DH, DH)]

    def moved(kind, source, target_slot, target):
        def copy(j, h):
            from_ref = other.at[j, h] if source is None else slot(j, h, source)
            return pltpu.make_async_remote_copy(
                src_ref=from_ref, dst_ref=slot(j, h, target_slot), send_sem=g_send.at[kind, j, h],
                recv_sem=g_recv.at[kind, j, h], device_id=target, device_id_type=MESH,
            )

        return copy

    own_to_sibling = moved(0, 0, 1, sibling_id)
    own_to_pair = moved(1, 0, 2, pair_id)
    pair_to_sibling = moved(2, 2, 3, sibling_id)
    other_to_across = moved(3, None, 4, across_id)
    across_to_sibling = moved(4, 4, 5, sibling_id)
    across_to_pair = moved(5, 4, 6, pair_id)
    far_to_sibling = moved(6, 6, 7, sibling_id)
    moves = (
        own_to_sibling, own_to_pair, pair_to_sibling, other_to_across,
        across_to_sibling, across_to_pair, far_to_sibling,
    )

    def mine_rows(j):
        return pl.ds(pl.multiple_of((mine * HALF + j) * CHUNK, CHUNK), CHUNK)

    def result_to_across(j):
        return pltpu.make_async_remote_copy(
            src_ref=staged.at[j], dst_ref=out.at[mine_rows(j), :], send_sem=out_send.at[j],
            recv_sem=out_recv.at[j], device_id=across_id, device_id_type=MESH,
        )

    def normed(u, h):
        value = local_out[u, :, h * DH : (h + 1) * DH] + dot(cross_lhs[u, h], cross_states[h])
        square = jnp.mean(value * value, axis=1, keepdims=True)
        return (value * lax.rsqrt(square + EPSILON)).astype(BF16)

    def finish(h):
        def step(j, carry):
            other[j, h] = normed((1 - mine) * HALF + j, h)
            other_to_across(j, h).start()
            gathered[j, h, :, 0:DH] = normed(mine * HALF + j, h)
            if h == 0:
                own_to_pair(j, h).start()
            own_to_sibling(j, h).start()
            return carry

        lax.fori_loop(0, HALF, step, 0)

    receive_y(0)
    finish(0)
    receive_y(1)
    finish(1)

    def forward(j, carry):
        own_to_pair(j, 1).start()
        for h in range(HEADS):
            other_to_across(j, h).wait_recv()
            across_to_pair(j, h).start()
            across_to_sibling(j, h).start()
        return carry

    lax.fori_loop(0, HALF, forward, 0)
    for copy in weight_sends:
        copy.wait_recv()

    for_own, for_across = (0, 1, 1, 0), (1, 0, 0, 1)

    def project(j, carry):
        def product(a, r):
            return sum(
                dot(gathered[j, h, :, r * 256 : (r + 1) * 256], weights[r, a[r], h].reshape(256, 256))
                for h in range(HEADS)
            )

        for h in range(HEADS):
            own_to_sibling(j, h).wait_recv()
            across_to_sibling(j, h).wait_recv()
            own_to_pair(j, h).wait_recv()
            pair_to_sibling(j, h).start()
        to_across = product(for_across, 0) + product(for_across, 2)
        to_own = product(for_own, 0) + product(for_own, 2)
        for h in range(HEADS):
            across_to_pair(j, h).wait_recv()
            far_to_sibling(j, h).start()
        for h in range(HEADS):
            pair_to_sibling(j, h).wait_recv()
        to_across += product(for_across, 1)
        to_own += product(for_own, 1)
        for h in range(HEADS):
            far_to_sibling(j, h).wait_recv()
        staged[j] = (to_across + product(for_across, 3)).astype(BF16)
        result_to_across(j).start()
        out[mine_rows(j), :] = (to_own + product(for_own, 3)).astype(BF16)
        return carry

    lax.fori_loop(0, HALF, project, 0)

    def drain(j, carry):
        for copy in moves:
            for h in range(HEADS):
                copy(j, h).wait_send()
        result_to_across(j).wait()
        return carry

    lax.fori_loop(0, HALF, drain, 0)
    for copy in sibling_pieces + weight_sends:
        copy.wait_send()
    for h in range(HEADS):
        for b in range(CTX_Z + PLACES_Y - 1):
            state_copy(h, b).wait_send()


def shards(tokens, w_query, w_key, w_value, w_out, decay_rate, level_row_index, level_weight_table):
    rows, depth = tokens.shape
    width = w_query.shape[1]
    vmem = functools.partial(pltpu.VMEM)
    dma = pltpu.SemaphoreType.DMA
    hbm, on_chip = pl.BlockSpec(memory_space=pl.ANY), pl.BlockSpec(memory_space=pltpu.VMEM)
    call = pl.pallas_call(
        kernel,
        out_shape=pltpu.VMEM((rows, width), BF16),
        in_specs=[hbm] * 5 + [on_chip] * 3,
        out_specs=on_chip,
        scratch_shapes=[
            vmem((rows, depth), BF16),
            vmem((HEADS, depth, 2 * DH), BF16),
            vmem((depth, width), BF16),
            vmem((HEADS, CHUNKS, CHUNK, 2 * DH), BF16),
            vmem((HEADS, CHUNKS, LOCAL * DH, DH), BF16),
            vmem((CHUNKS, CHUNK, width), F32),
            vmem((CHUNKS, HEADS, CHUNK, CROSS * DH), BF16),
            vmem((HEADS, CROSS * DH, DH), BF16),
            vmem((HEADS * ROWS, level_weight_table.shape[0]), F32),
            vmem((3, HEADS * ROWS, level_weight_table.shape[0]), BF16),
            vmem((HEADS * CHUNKS, CHUNK), F32),
            vmem((HEADS * CHUNKS, CHUNK), F32),
            vmem((HEADS * CHUNKS, ROWS, 128), F32),
            vmem((HEADS, CTX_Z + 1, MSG, DH), BF16),
            vmem((HEADS, CTX_Z + PLACES_Y - 1, MSG, DH), BF16),
            vmem((HALF, HEADS, CHUNK, 8 * DH), BF16),
            vmem((HALF, HEADS, CHUNK, DH), BF16),
            vmem((4, 2, HEADS, 2, DH, width), BF16),
            vmem((2, HEADS, 2, DH, width), BF16),
            vmem((HALF, CHUNK, width), BF16),
            dma((CHUNKS,)), dma((5,)), dma((4,)), dma((4,)), dma((4,)), dma((3,)), dma((3,)),
            dma((HEADS, CTX_Z + PLACES_Y - 1)), dma((HEADS, CTX_Z + PLACES_Y - 1)),
            dma((7, HALF, HEADS)), dma((7, HALF, HEADS)), dma((HALF,)), dma((HALF,)),
        ],
        compiler_params=pltpu.CompilerParams(
            collective_id=0, has_side_effects=True, vmem_limit_bytes=56 * 2**20
        ),
    )
    return call(
        tokens, w_query, w_key, w_value, w_out.reshape(HEADS, DH, -1), decay_rate.T, level_row_index.reshape(1, rows),
        level_weight_table.transpose(2, 1, 0),
    )


def solution(mesh):
    placed = (
        P("ctx", None),
        P(None, "head"),
        P(None, "head"),
        P(None, "head"),
        P("head", None),
        P("ctx", "head"),
        P("ctx"),
        P(None, "head", None),
    )
    return jax.shard_map(
        shards, mesh=mesh, in_specs=placed, out_specs=P("ctx", "head"), check_vma=False
    )
```

```python
import functools

import jax
import jax.numpy as jnp
from jax import lax
from jax.experimental import pallas as pl
from jax.experimental.pallas import tpu as pltpu
from jax.sharding import PartitionSpec as P

F32, BF16 = jnp.float32, jnp.bfloat16
MESH = pl.DeviceIdType.MESH
EPSILON = 1e-06
DH = 128
HEADS = 2
CHUNK = 256
CHUNKS = 8
HALF = CHUNKS // 2
PIECE = 128
PIECES = HALF * CHUNK // PIECE
LAG = 4
LOCAL = 3
PLACES_Z, PLACES_Y = 8, 4
CTX_Z, CTX_Y = 3, 2
CROSS = CTX_Z + CTX_Y
TALL = 2
FIRST_LOCAL, FIRST_CROSS = 3, 6
ROWS = 16
CUM = 11
MSG = DH + 16
NEVER = -1e30


def dot(a, b, dims=((1,), (0,))):
    return lax.dot_general(a, b, (dims, ((), ())), preferred_element_type=F32)


def split(x, terms):
    parts = []
    for _ in range(terms):
        part = x.astype(BF16)
        parts.append(part)
        x = x - part.astype(F32)
    return parts


def kernel(
    tokens, w_query, w_key, w_value, w_out, rates, row_index, table,
    out,
    tok, wkv, wq, kv, local_states, local_out, cross_lhs, cross_states,
    table_rows, table_parts, rate_rows, cum_rows, offset_rows, send_state, recv_state,
    gathered, other, weights, spare, partial, their_partial, own_partial, staged,
    tok_sem, w_sem, wl_sem, wx_send, wx_recv,
    st_send, st_recv, g_send, g_recv, p_send, p_recv, out_send, out_recv,
):
    pos = lax.axis_index("ctx")
    me = lax.axis_index("head")
    x = lax.div(me, 2)
    core = lax.rem(me, 2)
    pair = x + 1 - 2 * lax.rem(x, 2)
    across = 3 - x
    far = lax.rem(x + 2, 4)
    z = lax.rem(pos, PLACES_Z)
    y = lax.div(pos, PLACES_Z)
    sibling_id = (pos, 2 * x + 1 - core)
    pair_id = (pos, 2 * pair + core)
    across_id = (pos, 2 * across + core)
    far_id = (pos, 2 * far + core)
    z_bits = [lax.rem(lax.div(z, 2**b), 2) for b in range(CTX_Z)]
    flips = [2**b * (1 - 2 * z_bits[b]) for b in range(CTX_Z)]
    state_ids = [(pos + shift, me) for shift in (flips[0], flips[1], flips[1] + flips[2])]
    state_ids += [(lax.rem(y + d, PLACES_Y) * PLACES_Z + z, me) for d in range(1, PLACES_Y)]
    partners = [sibling_id, pair_id, across_id, far_id] + state_ids

    barrier = pltpu.get_barrier_semaphore()
    for partner in partners:
        pl.semaphore_signal(barrier, inc=1, device_id=partner, device_id_type=MESH)

    def weight_copy(source, head, part):
        return pltpu.make_async_copy(
            source.at[:, pl.ds(head * DH, DH)],
            wkv.at[head, :, pl.ds(part * DH, DH)],
            w_sem.at[head * 2 + part],
        )

    def token_rows(u, count):
        return pl.ds(pl.multiple_of(u * CHUNK, CHUNK), count * CHUNK)

    def token_copy(u):
        return pltpu.make_async_copy(
            tokens.at[token_rows(u, 1), :], tok.at[token_rows(u, 1), :], tok_sem.at[u]
        )

    query_copy = pltpu.make_async_copy(w_query, wq, w_sem.at[4])
    weight_copy(w_key, 0, 0).start()
    weight_copy(w_value, 0, 1).start()
    for u in range(CHUNKS):
        token_copy(u).start()

    homes = [(weights.at[0], 0, x), (weights.at[0], 1, across), (spare, 0, far), (spare, 1, pair)]
    own_pieces = []
    for i, (buffer, a, chip) in enumerate(homes):
        for k, side in enumerate((core, 1 - core)):
            columns = pl.ds(pl.multiple_of((2 * chip + side) * 256, 256), 256)
            own_pieces.append(
                pltpu.make_async_copy(w_out.at[:, columns], buffer.at[2 * a + k], wl_sem.at[2 * i + k])
            )

    def weight_send(i, source, target_ref, target):
        return pltpu.make_async_remote_copy(
            src_ref=source, dst_ref=target_ref, send_sem=wx_send.at[i],
            recv_sem=wx_recv.at[i], device_id=target, device_id_type=MESH,
        )

    weight_sends = [
        weight_send(0, spare.at[y], weights.at[3, y], far_id),
        weight_send(1, weights.at[0], weights.at[2], across_id),
        weight_send(2, spare, weights.at[1], pair_id),
    ]
    far_sends = [
        weight_send(2 + d, weights.at[3, y], weights.at[3, y], state_ids[CTX_Z + d - 1])
        for d in range(1, PLACES_Y)
    ]

    for u in range(CHUNKS):
        rate_rows[HEADS * u : HEADS * (u + 1), :] = rates[:, u * CHUNK : (u + 1) * CHUNK]
    before = lax.broadcasted_iota(jnp.int32, (CHUNK, CHUNK), 0)
    after = lax.broadcasted_iota(jnp.int32, (CHUNK, CHUNK), 1)
    upper = (before <= after).astype(BF16)
    cum = sum(dot(part, upper) for part in split(-rate_rows[...], 3))
    cum_rows[...] = cum
    last = cum[:, CHUNK - 1 :]
    key_decay = jnp.exp(last - cum).T
    totals = [[last[HEADS * u + h : HEADS * u + h + 1, :] for u in range(CHUNKS)] for h in range(HEADS)]

    table_rows[...] = jnp.zeros_like(table_rows)
    levels = table.shape[0]
    for h in range(HEADS):
        table_rows[h * ROWS : h * ROWS + levels, :] = table[:, h, :]
    for i, part in enumerate(split(table_rows[...], 3)):
        table_parts[i] = part
    level = lax.broadcasted_iota(jnp.int32, (ROWS, 128), 0)
    none = jnp.zeros((1, 1), F32)
    for u in range(CHUNKS):
        for h in range(HEADS):
            offset = jnp.where(level >= FIRST_CROSS, sum(totals[h][:u], none), none)
            ends = [none, totals[h][u - 1] if u % 2 else none, sum(totals[h][4:u], none)]
            for bit in range(LOCAL):
                end = ends[bit] if (u >> bit) & 1 else NEVER
                offset = jnp.where(level == FIRST_LOCAL + bit, end, offset)
            offset_rows[HEADS * u + h] = offset

    def key_value(h, i):
        result = dot(tok[token_rows(i * TALL, TALL), :], wkv[h]).astype(BF16)
        for part in range(TALL):
            kv[h, i * TALL + part] = result[part * CHUNK : (part + 1) * CHUNK]

    def chunk_state(h, u):
        decay = key_decay[:, HEADS * u + h : HEADS * u + h + 1]
        decayed = (kv[h, u, :, :DH].astype(F32) * decay).astype(BF16)
        return dot(decayed, kv[h, u, :, DH:], ((0,), (0,)))

    def merge(first, second):
        return jnp.exp(second[1]) * first[0] + second[0], first[1] + second[1]

    running = [None] * HEADS
    passed = [jnp.zeros((1, 1), F32) for _ in range(HEADS)]

    def state_copy(h, b):
        return pltpu.make_async_remote_copy(
            src_ref=send_state.at[h, min(b, CTX_Z)], dst_ref=recv_state.at[h, b], send_sem=st_send.at[h, b],
            recv_sem=st_recv.at[h, b], device_id=state_ids[b], device_id_type=MESH,
        )

    def send(h, b):
        state, total = running[h]
        send_state[h, b, 0:DH, :] = state.astype(BF16)
        row = lax.broadcasted_iota(jnp.int32, (16, DH), 0)
        tail = jnp.zeros((16, DH), F32)
        for i, part in enumerate(split(total, 3)):
            tail = jnp.where(row == i, part.astype(F32), tail)
        send_state[h, b, DH:MSG, :] = tail.astype(BF16)
        for step in [b] if b < CTX_Z else range(CTX_Z, CTX_Z + PLACES_Y - 1):
            state_copy(h, step).start()

    def arrived(h, b):
        state_copy(h, b).wait_recv()
        tail = recv_state[h, b, DH:MSG, :].astype(F32)
        return recv_state[h, b, 0:DH, :].astype(F32), tail[0:1, 0:1] + tail[1:2, 0:1] + tail[2:3, 0:1]

    def keep_cross(h, b, state):
        cross_states[h, b * DH : (b + 1) * DH, :] = state.astype(BF16)

    def receive_z(h, b):
        there, there_total = arrived(h, b)
        is_upper = z_bits[b] == 1
        state, total = running[h]
        low = jnp.where(is_upper, there, state)
        high = jnp.where(is_upper, state, there)
        high_total = jnp.where(is_upper, total, there_total)
        running[h] = (jnp.exp(high_total) * low + high, total + there_total)
        send(h, b + 1)
        keep_cross(h, b, jnp.where(is_upper, jnp.exp(passed[h]) * there, 0.0))
        passed[h] = passed[h] + jnp.where(is_upper, there_total, 0.0)

    def receive_y(h):
        behind = [arrived(h, CTX_Z + d) for d in range(PLACES_Y - 1)]
        is_odd, is_upper = lax.rem(y, 2) == 1, lax.div(y, 2) == 1
        (one, one_total), (two, two_total), (three, _) = behind
        keep_cross(h, CTX_Z, jnp.where(is_odd, jnp.exp(passed[h]) * one, 0.0))
        first, second = jnp.where(is_odd, three, two), jnp.where(is_odd, two, one)
        second_total = jnp.where(is_odd, two_total, one_total)
        ahead = passed[h] + jnp.where(is_odd, one_total, 0.0)
        both = jnp.exp(ahead) * (jnp.exp(second_total) * first + second)
        keep_cross(h, CTX_Z + 1, jnp.where(is_upper, both, 0.0))

    def own_state(h):
        single = [(chunk_state(h, u), totals[h][u]) for u in range(CHUNKS)]
        pairs = [merge(single[2 * i], single[2 * i + 1]) for i in range(4)]
        quads = [merge(pairs[2 * i], pairs[2 * i + 1]) for i in range(2)]
        running[h] = merge(quads[0], quads[1])
        send(h, 0)
        zero = jnp.zeros((DH, DH), BF16)
        for u in range(CHUNKS):
            lower = [
                single[u - 1][0].astype(BF16) if u & 1 else zero,
                pairs[u // 2 - 1][0].astype(BF16) if u & 2 else zero,
                quads[0][0].astype(BF16) if u & 4 else zero,
            ]
            for i, state in enumerate(lower):
                local_states[h, u, i * DH : (i + 1) * DH, :] = state

    weight_copy(w_key, 0, 0).wait()
    weight_copy(w_value, 0, 1).wait()

    def first_head(i, carry):
        for part in range(TALL):
            token_copy(i * TALL + part).wait()
        key_value(0, i)
        return carry

    def second_head(i, carry):
        key_value(1, i)
        return carry

    for copy in own_pieces:
        copy.start()
    weight_copy(w_key, 1, 0).start()
    weight_copy(w_value, 1, 1).start()
    query_copy.start()
    lax.fori_loop(0, 1, first_head, 0)
    pl.semaphore_wait(barrier, len(partners))
    lax.fori_loop(1, 3, first_head, 0)
    for copy in own_pieces:
        copy.wait()
    for copy in weight_sends:
        copy.start()
    lax.fori_loop(3, CHUNKS // TALL, first_head, 0)
    own_state(0)

    weight_copy(w_key, 1, 0).wait()
    weight_copy(w_value, 1, 1).wait()
    lax.fori_loop(0, CHUNKS // TALL, second_head, 0)
    receive_z(0, 0)
    own_state(1)
    query_copy.wait()
    weight_sends[0].wait_recv()
    for copy in far_sends:
        copy.start()

    def local_part(u, carry):
        queries = dot(tok[token_rows(u, 1), :], wq[...]).astype(BF16)
        slots = table.shape[2]
        chosen = lax.broadcasted_iota(jnp.int32, (slots, CHUNK), 0) == row_index[:, token_rows(u, 1)]
        chosen = jnp.where(chosen, 1.0, 0.0).astype(BF16)
        level_mix = sum(dot(table_parts[i], chosen) for i in range(3))
        row = lax.broadcasted_iota(jnp.int32, (ROWS, CHUNK), 0)
        rows = []
        for h in range(HEADS):
            cum_row = cum_rows[pl.ds(HEADS * u + h, 1), :]
            decay = cum_row + offset_rows[HEADS * u + h][:, 0:1]
            factor = jnp.exp(jnp.where(row >= FIRST_LOCAL, decay, 0.0))
            scaled = level_mix[h * ROWS : (h + 1) * ROWS, :] * factor
            rows.append(jnp.where(row == CUM, cum_row, scaled))
        cols = jnp.concatenate(rows, axis=0).T
        cols16 = cols.astype(BF16)
        token = lax.broadcasted_iota(jnp.int32, (CHUNK, CHUNK), 0)
        source = lax.broadcasted_iota(jnp.int32, (CHUNK, CHUNK), 1)
        causal = token >= source
        same_block = lax.div(token, 64) == lax.div(source, 64)
        same_pair = lax.div(token, 128) == lax.div(source, 128)
        for h in range(HEADS):
            column = lambda row: cols[:, h * ROWS + row : h * ROWS + row + 1]
            query = queries[:, h * DH : (h + 1) * DH]
            key, value = kv[h, u, :, 0:DH], kv[h, u, :, DH : 2 * DH]
            gap = column(CUM) - cum_rows[pl.ds(HEADS * u + h, 1), :]
            decay = jnp.exp(jnp.where(causal, gap, NEVER))
            mix = jnp.where(same_block, column(0), jnp.where(same_pair, column(1), column(2)))
            scores = dot(query, key, ((1,), (1,)))
            result = dot((scores * decay * mix).astype(BF16), value)
            column16 = lambda row: cols16[:, h * ROWS + row : h * ROWS + row + 1]
            lhs = [query * column16(FIRST_LOCAL + i) for i in range(LOCAL)]
            result += dot(jnp.concatenate(lhs, axis=1), local_states[h, u])
            local_out[u, :, h * DH : (h + 1) * DH] = result
            for i in range(CROSS):
                cross_lhs[u, h, :, i * DH : (i + 1) * DH] = query * column16(FIRST_CROSS + i)
        return carry

    lax.fori_loop(0, 2, local_part, 0)
    receive_z(0, 1)
    receive_z(1, 0)
    lax.fori_loop(2, 5, local_part, 0)
    receive_z(0, 2)
    receive_z(1, 1)
    lax.fori_loop(5, CHUNKS, local_part, 0)

    mine = lax.div(x, 2)

    def moved(kind, source, target_slot, target):
        def copy(j, h):
            return pltpu.make_async_remote_copy(
                src_ref=other.at[j, h] if source is None else gathered.at[j, h, source],
                dst_ref=gathered.at[j, h, target_slot], send_sem=g_send.at[kind, j, h],
                recv_sem=g_recv.at[kind, j, h], device_id=target, device_id_type=MESH,
            )

        return copy

    own_to_pair = moved(0, 0, 1, pair_id)
    other_to_across = moved(1, None, 2, across_id)
    across_to_pair = moved(2, 2, 3, pair_id)

    def partial_to_sibling(j):
        return pltpu.make_async_remote_copy(
            src_ref=partial.at[j], dst_ref=their_partial.at[j], send_sem=p_send.at[j],
            recv_sem=p_recv.at[j], device_id=sibling_id, device_id_type=MESH,
        )

    def mine_rows(j):
        return pl.ds(pl.multiple_of((mine * PIECES + j) * PIECE, PIECE), PIECE)

    def result_to_across(j):
        return pltpu.make_async_remote_copy(
            src_ref=staged.at[j], dst_ref=out.at[mine_rows(j), :], send_sem=out_send.at[j],
            recv_sem=out_recv.at[j], device_id=across_id, device_id_type=MESH,
        )

    def normed(u, h):
        value = local_out[u, :, h * DH : (h + 1) * DH] + dot(cross_lhs[u, h], cross_states[h])
        square = jnp.mean(value * value, axis=1, keepdims=True)
        return (value * lax.rsqrt(square + EPSILON)).astype(BF16)

    def finish(h):
        def step(j, carry):
            theirs = normed((1 - mine) * HALF + j, h)
            for part in range(CHUNK // PIECE):
                here = j * (CHUNK // PIECE) + part
                other[here, h] = theirs[part * PIECE : (part + 1) * PIECE]
                other_to_across(here, h).start()
            ours = normed(mine * HALF + j, h)
            for part in range(CHUNK // PIECE):
                here = j * (CHUNK // PIECE) + part
                gathered[here, h, 0] = ours[part * PIECE : (part + 1) * PIECE]
                if h == 0:
                    own_to_pair(here, h).start()
            return carry

        lax.fori_loop(0, HALF, step, 0)

    receive_y(0)
    receive_z(1, 2)
    finish(0)
    receive_y(1)
    finish(1)

    for_own, for_across = (0, 1, 1, 0), (1, 0, 0, 1)

    def forward(j):
        own_to_pair(j, 1).start()
        for h in range(HEADS):
            other_to_across(j, h).wait_recv()
            across_to_pair(j, h).start()

    def project(j):
        def product(r, a, k):
            both = jnp.concatenate([gathered[j, h, r] for h in range(HEADS)], axis=1)
            return dot(both, weights[r, 2 * a[r] + k])

        for h in range(HEADS):
            own_to_pair(j, h).wait_recv()
            across_to_pair(j, h).wait_recv()
        for k in (1, 0):
            for i, a in enumerate((for_across, for_own)):
                result = sum(product(r, a, k) for r in range(4))
                if k == 1:
                    partial[j, i] = result.astype(BF16)
                else:
                    own_partial[j, i] = result
            if k == 1:
                partial_to_sibling(j).start()

    def deliver(j):
        partial_to_sibling(j).wait_recv()
        staged[j] = (own_partial[j, 0] + their_partial[j, 0].astype(F32)).astype(BF16)
        result_to_across(j).start()
        out[mine_rows(j), :] = (own_partial[j, 1] + their_partial[j, 1].astype(F32)).astype(BF16)

    def step(j, carry):
        @pl.when(j < PIECES)
        def _():
            forward(j)

        @pl.when(j == LAG)
        def _():
            for copy in weight_sends[1:] + far_sends:
                copy.wait_recv()

        @pl.when((j >= LAG) & (j < PIECES + LAG))
        def _():
            project(j - LAG)

        @pl.when(j > LAG)
        def _():
            deliver(j - LAG - 1)

        return carry

    lax.fori_loop(0, PIECES + LAG + 1, step, 0)

    def drain(j, carry):
        for copy in (own_to_pair, other_to_across, across_to_pair):
            for h in range(HEADS):
                copy(j, h).wait_send()
        partial_to_sibling(j).wait_send()
        result_to_across(j).wait()
        return carry

    lax.fori_loop(0, PIECES, drain, 0)
    for copy in weight_sends + far_sends:
        copy.wait_send()
    for h in range(HEADS):
        for b in range(CTX_Z + PLACES_Y - 1):
            state_copy(h, b).wait_send()


def shards(tokens, w_query, w_key, w_value, w_out, decay_rate, level_row_index, level_weight_table):
    rows, depth = tokens.shape
    width = w_query.shape[1]
    vmem = functools.partial(pltpu.VMEM)
    dma = pltpu.SemaphoreType.DMA
    hbm, on_chip = pl.BlockSpec(memory_space=pl.ANY), pl.BlockSpec(memory_space=pltpu.VMEM)
    call = pl.pallas_call(
        kernel,
        out_shape=pltpu.VMEM((rows, width), BF16),
        in_specs=[hbm] * 5 + [on_chip] * 3,
        out_specs=on_chip,
        scratch_shapes=[
            vmem((rows, depth), BF16),
            vmem((HEADS, depth, 2 * DH), BF16),
            vmem((depth, width), BF16),
            vmem((HEADS, CHUNKS, CHUNK, 2 * DH), BF16),
            vmem((HEADS, CHUNKS, LOCAL * DH, DH), BF16),
            vmem((CHUNKS, CHUNK, width), F32),
            vmem((CHUNKS, HEADS, CHUNK, CROSS * DH), BF16),
            vmem((HEADS, CROSS * DH, DH), BF16),
            vmem((HEADS * ROWS, level_weight_table.shape[0]), F32),
            vmem((3, HEADS * ROWS, level_weight_table.shape[0]), BF16),
            vmem((HEADS * CHUNKS, CHUNK), F32),
            vmem((HEADS * CHUNKS, CHUNK), F32),
            vmem((HEADS * CHUNKS, ROWS, 128), F32),
            vmem((HEADS, CTX_Z + 1, MSG, DH), BF16),
            vmem((HEADS, CTX_Z + PLACES_Y - 1, MSG, DH), BF16),
            vmem((PIECES, HEADS, 4, PIECE, DH), BF16),
            vmem((PIECES, HEADS, PIECE, DH), BF16),
            vmem((4, 4, width, width), BF16),
            vmem((4, width, width), BF16),
            vmem((PIECES, 2, PIECE, width), BF16),
            vmem((PIECES, 2, PIECE, width), BF16),
            vmem((PIECES, 2, PIECE, width), F32),
            vmem((PIECES, PIECE, width), BF16),
            dma((CHUNKS,)), dma((5,)), dma((8,)), dma((6,)), dma((6,)),
            dma((HEADS, CTX_Z + PLACES_Y - 1)), dma((HEADS, CTX_Z + PLACES_Y - 1)),

            dma((3, PIECES, HEADS)), dma((3, PIECES, HEADS)),
            dma((PIECES,)), dma((PIECES,)), dma((PIECES,)), dma((PIECES,)),
        ],
        compiler_params=pltpu.CompilerParams(
            collective_id=0, has_side_effects=True, vmem_limit_bytes=56 * 2**20
        ),
    )
    return call(
        tokens, w_query, w_key, w_value, w_out, decay_rate.T, level_row_index.reshape(1, rows),
        level_weight_table.transpose(2, 1, 0),
    )


def solution(mesh):
    placed = (
        P("ctx", None),
        P(None, "head"),
        P(None, "head"),
        P(None, "head"),
        P("head", None),
        P("ctx", "head"),
        P("ctx"),
        P(None, "head", None),
    )
    return jax.shard_map(
        shards, mesh=mesh, in_specs=placed, out_specs=P("ctx", "head"), check_vma=False
    )
```

```python
import functools

import jax
import jax.numpy as jnp
from jax import lax
from jax.experimental import pallas as pl
from jax.experimental.pallas import tpu as pltpu
from jax.sharding import PartitionSpec as P

F32, BF16 = jnp.float32, jnp.bfloat16
MESH = pl.DeviceIdType.MESH
EPSILON = 1e-06
DH = 128
HEADS = 2
CHUNK = 256
CHUNKS = 8
HALF = CHUNKS // 2
PIECE = 128
PIECES = HALF * CHUNK // PIECE
LAST, EXTRA = PIECES - 1, PIECES
LAG = 3
LOCAL = 3
PLACES_Z, PLACES_Y = 8, 4
CTX_Z, CTX_Y = 3, 2
CROSS = CTX_Z + CTX_Y
TALL = 2
FIRST_LOCAL, FIRST_CROSS = 3, 6
ROWS = 16
CUM = 11
MSG = DH + 16
NEVER = -1e30


def dot(a, b, dims=((1,), (0,))):
    return lax.dot_general(a, b, (dims, ((), ())), preferred_element_type=F32)


def split(x, terms):
    parts = []
    for _ in range(terms):
        part = x.astype(BF16)
        parts.append(part)
        x = x - part.astype(F32)
    return parts


def kernel(
    tokens, w_query, w_key, w_value, w_out, rates_in, row_index_in, table_in,
    out,
    rates, row_index, table, small_sem,
    tok, wkv, wq, kv, local_states, local_out, cross_lhs, cross_states,
    table_rows, table_parts, rate_rows, cum_rows, offset_rows, send_state, recv_state,
    gathered, other, weights, spare, partial, their_partial, own_partial, staged,
    tok_sem, w_sem, wl_sem, wx_send, wx_recv,
    st_send, st_recv, g_send, g_recv, x_send, x_recv, p_send, p_recv, out_send, out_recv,
):
    pos = lax.axis_index("ctx")
    me = lax.axis_index("head")
    x = lax.div(me, 2)
    core = lax.rem(me, 2)
    pair = x + 1 - 2 * lax.rem(x, 2)
    across = 3 - x
    far = lax.rem(x + 2, 4)
    z = lax.rem(pos, PLACES_Z)
    y = lax.div(pos, PLACES_Z)
    sibling_id = (pos, 2 * x + 1 - core)
    pair_id = (pos, 2 * pair + core)
    across_id = (pos, 2 * across + core)
    far_id = (pos, 2 * far + core)
    z_bits = [lax.rem(lax.div(z, 2**b), 2) for b in range(CTX_Z)]
    flips = [2**b * (1 - 2 * z_bits[b]) for b in range(CTX_Z)]
    state_ids = [(pos + shift, me) for shift in (flips[0], flips[1], flips[1] + flips[2])]
    state_ids += [(lax.rem(y + d, PLACES_Y) * PLACES_Z + z, me) for d in range(1, PLACES_Y)]
    partners = [sibling_id, pair_id, across_id, far_id] + state_ids

    barrier = pltpu.get_barrier_semaphore()
    for partner in partners:
        pl.semaphore_signal(barrier, inc=1, device_id=partner, device_id_type=MESH)

    def weight_copy(source, head, part):
        return pltpu.make_async_copy(
            source.at[:, pl.ds(head * DH, DH)],
            wkv.at[head, :, pl.ds(part * DH, DH)],
            w_sem.at[head * 2 + part],
        )

    def token_rows(u, count):
        return pl.ds(pl.multiple_of(u * CHUNK, CHUNK), count * CHUNK)

    def token_copy(u):
        return pltpu.make_async_copy(
            tokens.at[token_rows(u, 1), :], tok.at[token_rows(u, 1), :], tok_sem.at[u]
        )

    small = [
        pltpu.make_async_copy(source, target, small_sem.at[i])
        for i, (source, target) in enumerate(((rates_in, rates), (row_index_in, row_index), (table_in, table)))
    ]
    for copy in small:
        copy.start()
    query_copy = pltpu.make_async_copy(w_query, wq, w_sem.at[4])
    weight_copy(w_key, 0, 0).start()
    weight_copy(w_value, 0, 1).start()
    for u in range(CHUNKS):
        token_copy(u).start()

    homes = [(weights.at[0], 0, x), (weights.at[0], 1, across), (spare, 0, far), (spare, 1, pair)]
    own_pieces = []
    for i, (buffer, a, chip) in enumerate(homes):
        for k, side in enumerate((core, 1 - core)):
            columns = pl.ds(pl.multiple_of((2 * chip + side) * 256, 256), 256)
            own_pieces.append(
                pltpu.make_async_copy(w_out.at[:, columns], buffer.at[2 * a + k], wl_sem.at[2 * i + k])
            )

    def weight_send(i, source, target_ref, target):
        return pltpu.make_async_remote_copy(
            src_ref=source, dst_ref=target_ref, send_sem=wx_send.at[i],
            recv_sem=wx_recv.at[i], device_id=target, device_id_type=MESH,
        )

    weight_sends = [
        weight_send(0, spare.at[y], weights.at[3, y], far_id),
        weight_send(1, weights.at[0], weights.at[2], across_id),
        weight_send(2, spare, weights.at[1], pair_id),
    ]
    far_sends = [
        weight_send(2 + d, weights.at[3, y], weights.at[3, y], state_ids[CTX_Z + d - 1])
        for d in range(1, PLACES_Y)
    ]

    for copy in small:
        copy.wait()

    for u in range(CHUNKS):
        rate_rows[HEADS * u : HEADS * (u + 1), :] = rates[:, u * CHUNK : (u + 1) * CHUNK]
    before = lax.broadcasted_iota(jnp.int32, (CHUNK, CHUNK), 0)
    after = lax.broadcasted_iota(jnp.int32, (CHUNK, CHUNK), 1)
    upper = (before <= after).astype(BF16)
    cum = sum(dot(part, upper) for part in split(-rate_rows[...], 3))
    cum_rows[...] = cum
    last = cum[:, CHUNK - 1 :]
    key_decay = jnp.exp(last - cum).T
    totals = [[last[HEADS * u + h : HEADS * u + h + 1, :] for u in range(CHUNKS)] for h in range(HEADS)]

    table_rows[...] = jnp.zeros_like(table_rows)
    levels = table.shape[0]
    for h in range(HEADS):
        table_rows[h * ROWS : h * ROWS + levels, :] = table[:, h, :]
    for i, part in enumerate(split(table_rows[...], 3)):
        table_parts[i] = part
    level = lax.broadcasted_iota(jnp.int32, (ROWS, 128), 0)
    none = jnp.zeros((1, 1), F32)
    for u in range(CHUNKS):
        for h in range(HEADS):
            offset = jnp.where(level >= FIRST_CROSS, sum(totals[h][:u], none), none)
            ends = [none, totals[h][u - 1] if u % 2 else none, sum(totals[h][4:u], none)]
            for bit in range(LOCAL):
                end = ends[bit] if (u >> bit) & 1 else NEVER
                offset = jnp.where(level == FIRST_LOCAL + bit, end, offset)
            offset_rows[HEADS * u + h] = offset

    def key_value(h, i):
        result = dot(tok[token_rows(i * TALL, TALL), :], wkv[h]).astype(BF16)
        for part in range(TALL):
            kv[h, i * TALL + part] = result[part * CHUNK : (part + 1) * CHUNK]

    def chunk_state(h, u):
        decay = key_decay[:, HEADS * u + h : HEADS * u + h + 1]
        decayed = (kv[h, u, :, :DH].astype(F32) * decay).astype(BF16)
        return dot(decayed, kv[h, u, :, DH:], ((0,), (0,)))

    def merge(first, second):
        return jnp.exp(second[1]) * first[0] + second[0], first[1] + second[1]

    running = [None] * HEADS
    passed = [jnp.zeros((1, 1), F32) for _ in range(HEADS)]

    def state_copy(h, b):
        return pltpu.make_async_remote_copy(
            src_ref=send_state.at[h, min(b, CTX_Z)], dst_ref=recv_state.at[h, b], send_sem=st_send.at[h, b],
            recv_sem=st_recv.at[h, b], device_id=state_ids[b], device_id_type=MESH,
        )

    def send(h, b):
        state, total = running[h]
        send_state[h, b, 0:DH, :] = state.astype(BF16)
        row = lax.broadcasted_iota(jnp.int32, (16, DH), 0)
        tail = jnp.zeros((16, DH), F32)
        for i, part in enumerate(split(total, 3)):
            tail = jnp.where(row == i, part.astype(F32), tail)
        send_state[h, b, DH:MSG, :] = tail.astype(BF16)
        for step in [b] if b < CTX_Z else range(CTX_Z, CTX_Z + PLACES_Y - 1):
            state_copy(h, step).start()

    def arrived(h, b):
        state_copy(h, b).wait_recv()
        tail = recv_state[h, b, DH:MSG, :].astype(F32)
        return recv_state[h, b, 0:DH, :].astype(F32), tail[0:1, 0:1] + tail[1:2, 0:1] + tail[2:3, 0:1]

    def keep_cross(h, b, state):
        cross_states[h, b * DH : (b + 1) * DH, :] = state.astype(BF16)

    def receive_z(h, b):
        there, there_total = arrived(h, b)
        is_upper = z_bits[b] == 1
        state, total = running[h]
        low = jnp.where(is_upper, there, state)
        high = jnp.where(is_upper, state, there)
        high_total = jnp.where(is_upper, total, there_total)
        running[h] = (jnp.exp(high_total) * low + high, total + there_total)
        send(h, b + 1)
        keep_cross(h, b, jnp.where(is_upper, jnp.exp(passed[h]) * there, 0.0))
        passed[h] = passed[h] + jnp.where(is_upper, there_total, 0.0)

    def receive_y(h):
        behind = [arrived(h, CTX_Z + d) for d in range(PLACES_Y - 1)]
        is_odd, is_upper = lax.rem(y, 2) == 1, lax.div(y, 2) == 1
        (one, one_total), (two, two_total), (three, _) = behind
        keep_cross(h, CTX_Z, jnp.where(is_odd, jnp.exp(passed[h]) * one, 0.0))
        first, second = jnp.where(is_odd, three, two), jnp.where(is_odd, two, one)
        second_total = jnp.where(is_odd, two_total, one_total)
        ahead = passed[h] + jnp.where(is_odd, one_total, 0.0)
        both = jnp.exp(ahead) * (jnp.exp(second_total) * first + second)
        keep_cross(h, CTX_Z + 1, jnp.where(is_upper, both, 0.0))

    def own_state(h):
        single = [(chunk_state(h, u), totals[h][u]) for u in range(CHUNKS)]
        pairs = [merge(single[2 * i], single[2 * i + 1]) for i in range(4)]
        quads = [merge(pairs[2 * i], pairs[2 * i + 1]) for i in range(2)]
        running[h] = merge(quads[0], quads[1])
        send(h, 0)
        zero = jnp.zeros((DH, DH), BF16)
        for u in range(CHUNKS):
            lower = [
                single[u - 1][0].astype(BF16) if u & 1 else zero,
                pairs[u // 2 - 1][0].astype(BF16) if u & 2 else zero,
                quads[0][0].astype(BF16) if u & 4 else zero,
            ]
            for i, state in enumerate(lower):
                local_states[h, u, i * DH : (i + 1) * DH, :] = state

    weight_copy(w_key, 0, 0).wait()
    weight_copy(w_value, 0, 1).wait()

    def first_head(i, carry):
        for part in range(TALL):
            token_copy(i * TALL + part).wait()
        key_value(0, i)
        return carry

    def second_head(i, carry):
        key_value(1, i)
        return carry

    for copy in own_pieces:
        copy.start()
    weight_copy(w_key, 1, 0).start()
    weight_copy(w_value, 1, 1).start()
    query_copy.start()
    lax.fori_loop(0, 1, first_head, 0)
    pl.semaphore_wait(barrier, len(partners))
    lax.fori_loop(1, 3, first_head, 0)
    for copy in own_pieces:
        copy.wait()
    for copy in weight_sends:
        copy.start()
    lax.fori_loop(3, CHUNKS // TALL, first_head, 0)
    own_state(0)

    weight_copy(w_key, 1, 0).wait()
    weight_copy(w_value, 1, 1).wait()
    lax.fori_loop(0, CHUNKS // TALL, second_head, 0)
    receive_z(0, 0)
    own_state(1)
    query_copy.wait()
    weight_sends[0].wait_recv()
    for copy in far_sends:
        copy.start()

    def local_part(u, carry):
        queries = dot(tok[token_rows(u, 1), :], wq[...]).astype(BF16)
        slots = table.shape[2]
        chosen = lax.broadcasted_iota(jnp.int32, (slots, CHUNK), 0) == row_index[:, token_rows(u, 1)]
        chosen = jnp.where(chosen, 1.0, 0.0).astype(BF16)
        level_mix = sum(dot(table_parts[i], chosen) for i in range(3))
        row = lax.broadcasted_iota(jnp.int32, (ROWS, CHUNK), 0)
        rows = []
        for h in range(HEADS):
            cum_row = cum_rows[pl.ds(HEADS * u + h, 1), :]
            decay = cum_row + offset_rows[HEADS * u + h][:, 0:1]
            factor = jnp.exp(jnp.where(row >= FIRST_LOCAL, decay, 0.0))
            scaled = level_mix[h * ROWS : (h + 1) * ROWS, :] * factor
            rows.append(jnp.where(row == CUM, cum_row, scaled))
        cols = jnp.concatenate(rows, axis=0).T
        cols16 = cols.astype(BF16)
        token = lax.broadcasted_iota(jnp.int32, (CHUNK, CHUNK), 0)
        source = lax.broadcasted_iota(jnp.int32, (CHUNK, CHUNK), 1)
        causal = token >= source
        same_block = lax.div(token, 64) == lax.div(source, 64)
        same_pair = lax.div(token, 128) == lax.div(source, 128)
        for h in range(HEADS):
            column = lambda row: cols[:, h * ROWS + row : h * ROWS + row + 1]
            query = queries[:, h * DH : (h + 1) * DH]
            key, value = kv[h, u, :, 0:DH], kv[h, u, :, DH : 2 * DH]
            gap = column(CUM) - cum_rows[pl.ds(HEADS * u + h, 1), :]
            decay = jnp.exp(jnp.where(causal, gap, NEVER))
            mix = jnp.where(same_block, column(0), jnp.where(same_pair, column(1), column(2)))
            scores = dot(query, key, ((1,), (1,)))
            result = dot((scores * decay * mix).astype(BF16), value)
            column16 = lambda row: cols16[:, h * ROWS + row : h * ROWS + row + 1]
            lhs = [query * column16(FIRST_LOCAL + i) for i in range(LOCAL)]
            result += dot(jnp.concatenate(lhs, axis=1), local_states[h, u])
            local_out[u, :, h * DH : (h + 1) * DH] = result
            for i in range(CROSS):
                cross_lhs[u, h, :, i * DH : (i + 1) * DH] = query * column16(FIRST_CROSS + i)
        return carry

    lax.fori_loop(0, 2, local_part, 0)
    receive_z(0, 1)
    receive_z(1, 0)
    lax.fori_loop(2, 5, local_part, 0)
    receive_z(0, 2)
    receive_z(1, 1)
    lax.fori_loop(5, CHUNKS, local_part, 0)

    mine = lax.div(x, 2)

    def moved(kind, source, target_slot, target):
        def copy(j, h):
            return pltpu.make_async_remote_copy(
                src_ref=other.at[j, h] if source is None else gathered.at[j, h, source],
                dst_ref=gathered.at[j, h, target_slot], send_sem=g_send.at[kind, j, h],
                recv_sem=g_recv.at[kind, j, h], device_id=target, device_id_type=MESH,
            )

        return copy

    own_to_pair = moved(0, 0, 1, pair_id)
    other_to_across = moved(1, None, 2, across_id)
    across_to_pair = moved(2, 2, 3, pair_id)

    def moved_extra(kind, piece, source, target_slot, target):
        def copy(h):
            return pltpu.make_async_remote_copy(
                src_ref=gathered.at[piece, h, source], dst_ref=gathered.at[EXTRA, h, target_slot],
                send_sem=x_send.at[kind, h], recv_sem=x_recv.at[kind, h],
                device_id=target, device_id_type=MESH,
            )

        return copy

    extra_to_pair = moved_extra(0, EXTRA, 0, 1, pair_id)
    last_to_across = moved_extra(1, LAST, 0, 2, across_id)
    last_pair_to_across = moved_extra(2, LAST, 1, 3, across_id)
    extra_moves = (extra_to_pair, last_to_across, last_pair_to_across)

    def partial_to_sibling(j):
        return pltpu.make_async_remote_copy(
            src_ref=partial.at[j], dst_ref=their_partial.at[j], send_sem=p_send.at[j],
            recv_sem=p_recv.at[j], device_id=sibling_id, device_id_type=MESH,
        )

    def mine_rows(j):
        return pl.ds(pl.multiple_of((mine * PIECES + j) * PIECE, PIECE), PIECE)

    def result_to_across(j):
        return pltpu.make_async_remote_copy(
            src_ref=staged.at[j], dst_ref=out.at[mine_rows(j), :], send_sem=out_send.at[j],
            recv_sem=out_recv.at[j], device_id=across_id, device_id_type=MESH,
        )

    def normed(u, h):
        value = local_out[u, :, h * DH : (h + 1) * DH] + dot(cross_lhs[u, h], cross_states[h])
        square = jnp.mean(value * value, axis=1, keepdims=True)
        return (value * lax.rsqrt(square + EPSILON)).astype(BF16)

    def finish(h):
        def step(j, carry):
            theirs = normed((1 - mine) * HALF + j, h)
            for part in range(CHUNK // PIECE):
                here = j * (CHUNK // PIECE) + part
                other[here, h] = theirs[part * PIECE : (part + 1) * PIECE]
                other_to_across(here, h).start()
            ours = normed(mine * HALF + j, h)
            for part in range(CHUNK // PIECE):
                here = j * (CHUNK // PIECE) + part
                gathered[here, h, 0] = ours[part * PIECE : (part + 1) * PIECE]
                if h == 0:
                    own_to_pair(here, h).start()
            return carry

        lax.fori_loop(0, HALF, step, 0)
        gathered[EXTRA, h, 0] = other[LAST, h]
        last_to_across(h).start()
        if h == 1:
            own_to_pair(LAST, h).start()

    receive_y(0)
    receive_z(1, 2)
    finish(0)
    receive_y(1)
    finish(1)

    for_own, for_across = (0, 1, 1, 0), (1, 0, 0, 1)

    def forward(j):
        @pl.when(j < LAST)
        def _():
            own_to_pair(j, 1).start()

        for h in range(HEADS):
            other_to_across(j, h).wait_recv()
            across_to_pair(j, h).start()

        @pl.when(j == LAST)
        def _():
            for h in range(HEADS):
                extra_to_pair(h).start()
                own_to_pair(LAST, h).wait_recv()
                last_pair_to_across(h).start()

    def product(j, a, k):
        def term(r):
            both = jnp.concatenate([gathered[j, h, r] for h in range(HEADS)], axis=1)
            return dot(both, weights[r, 2 * a[r] + k])

        return sum(term(r) for r in range(4))

    def project(j):
        for h in range(HEADS):
            own_to_pair(j, h).wait_recv()
            across_to_pair(j, h).wait_recv()
        for i, a in enumerate((for_across, for_own)):
            partial[j, i] = product(j, a, 1).astype(BF16)
        partial_to_sibling(j).start()
        for i, a in enumerate((for_across, for_own)):
            own_partial[j, i] = product(j, a, 0)

    def deliver(j):
        partial_to_sibling(j).wait_recv()
        staged[j] = (own_partial[j, 0] + their_partial[j, 0].astype(F32)).astype(BF16)
        result_to_across(j).start()
        out[mine_rows(j), :] = (own_partial[j, 1] + their_partial[j, 1].astype(F32)).astype(BF16)

    def step(j, carry):
        @pl.when(j < PIECES)
        def _():
            forward(j)

        @pl.when(j == LAG)
        def _():
            for copy in weight_sends[1:] + far_sends:
                copy.wait_recv()

        @pl.when((j >= LAG) & (j < LAST + LAG))
        def _():
            project(j - LAG)

        @pl.when(j > LAG)
        def _():
            deliver(j - LAG - 1)

        return carry

    lax.fori_loop(0, LAST + LAG + 1, step, 0)

    for h in range(HEADS):
        last_to_across(h).wait_recv()
        last_pair_to_across(h).wait_recv()
        across_to_pair(LAST, h).wait_recv()
        extra_to_pair(h).wait_recv()
    for i, piece in enumerate((EXTRA, LAST)):
        partial[LAST, i] = product(piece, for_own, 1).astype(BF16)
    partial_to_sibling(LAST).start()
    results = [product(piece, for_own, 0) for piece in (EXTRA, LAST)]
    partial_to_sibling(LAST).wait_recv()
    extra_rows = pl.ds(pl.multiple_of(((1 - mine) * PIECES + LAST) * PIECE, PIECE), PIECE)
    out[extra_rows, :] = (results[0] + their_partial[LAST, 0].astype(F32)).astype(BF16)
    out[mine_rows(LAST), :] = (results[1] + their_partial[LAST, 1].astype(F32)).astype(BF16)

    def drain(j, carry):
        for copy in (own_to_pair, other_to_across, across_to_pair):
            for h in range(HEADS):
                copy(j, h).wait_send()
        partial_to_sibling(j).wait_send()
        return carry

    def drain_results(j, carry):
        result_to_across(j).wait()
        return carry

    lax.fori_loop(0, PIECES, drain, 0)
    lax.fori_loop(0, LAST, drain_results, 0)
    for copy in extra_moves:
        for h in range(HEADS):
            copy(h).wait_send()
    for copy in weight_sends + far_sends:
        copy.wait_send()
    for h in range(HEADS):
        for b in range(CTX_Z + PLACES_Y - 1):
            state_copy(h, b).wait_send()


def shards(tokens, w_query, w_key, w_value, w_out, decay_rate, level_row_index, level_weight_table):
    rows, depth = tokens.shape
    width = w_query.shape[1]
    vmem = functools.partial(pltpu.VMEM)
    dma = pltpu.SemaphoreType.DMA
    hbm, on_chip = pl.BlockSpec(memory_space=pl.ANY), pl.BlockSpec(memory_space=pltpu.VMEM)
    call = pl.pallas_call(
        kernel,
        out_shape=pltpu.VMEM((rows, width), BF16),
        in_specs=[hbm] * 8,
        out_specs=on_chip,
        scratch_shapes=[
            vmem((HEADS, rows), F32),
            vmem((1, rows), jnp.int32),
            vmem(level_weight_table.shape[::-1], F32),
            dma((3,)),
            vmem((rows, depth), BF16),
            vmem((HEADS, depth, 2 * DH), BF16),
            vmem((depth, width), BF16),
            vmem((HEADS, CHUNKS, CHUNK, 2 * DH), BF16),
            vmem((HEADS, CHUNKS, LOCAL * DH, DH), BF16),
            vmem((CHUNKS, CHUNK, width), F32),
            vmem((CHUNKS, HEADS, CHUNK, CROSS * DH), BF16),
            vmem((HEADS, CROSS * DH, DH), BF16),
            vmem((HEADS * ROWS, level_weight_table.shape[0]), F32),
            vmem((3, HEADS * ROWS, level_weight_table.shape[0]), BF16),
            vmem((HEADS * CHUNKS, CHUNK), F32),
            vmem((HEADS * CHUNKS, CHUNK), F32),
            vmem((HEADS * CHUNKS, ROWS, 128), F32),
            vmem((HEADS, CTX_Z + 1, MSG, DH), BF16),
            vmem((HEADS, CTX_Z + PLACES_Y - 1, MSG, DH), BF16),
            vmem((PIECES + 1, HEADS, 4, PIECE, DH), BF16),
            vmem((PIECES, HEADS, PIECE, DH), BF16),
            vmem((4, 4, width, width), BF16),
            vmem((4, width, width), BF16),
            vmem((PIECES, 2, PIECE, width), BF16),
            vmem((PIECES, 2, PIECE, width), BF16),
            vmem((LAST, 2, PIECE, width), F32),
            vmem((LAST, PIECE, width), BF16),
            dma((CHUNKS,)), dma((5,)), dma((8,)), dma((6,)), dma((6,)),
            dma((HEADS, CTX_Z + PLACES_Y - 1)), dma((HEADS, CTX_Z + PLACES_Y - 1)),

            dma((3, PIECES, HEADS)), dma((3, PIECES, HEADS)), dma((3, HEADS)), dma((3, HEADS)),
            dma((PIECES,)), dma((PIECES,)), dma((LAST,)), dma((LAST,)),
        ],
        compiler_params=pltpu.CompilerParams(
            collective_id=0, has_side_effects=True, vmem_limit_bytes=56 * 2**20
        ),
    )
    return call(
        tokens, w_query, w_key, w_value, w_out, decay_rate.T, level_row_index.reshape(1, rows),
        level_weight_table.transpose(2, 1, 0),
    )


def solution(mesh):
    placed = (
        P("ctx", None),
        P(None, "head"),
        P(None, "head"),
        P(None, "head"),
        P("head", None),
        P("ctx", "head"),
        P("ctx"),
        P(None, "head", None),
    )
    return jax.shard_map(
        shards, mesh=mesh, in_specs=placed, out_specs=P("ctx", "head"), check_vma=False
    )
```

```python
import functools

import jax
import jax.numpy as jnp
from jax import lax
from jax.experimental import pallas as pl
from jax.experimental.pallas import tpu as pltpu
from jax.sharding import PartitionSpec as P

F32, BF16 = jnp.float32, jnp.bfloat16
MESH = pl.DeviceIdType.MESH
EPSILON = 1e-06
DH = 128
HEADS = 2
CHUNK = 256
CHUNKS = 8
HALF = CHUNKS // 2
PIECE = 128
PIECES = HALF * CHUNK // PIECE
LAST, EXTRA = PIECES - 1, PIECES
LAG = 3
LOCAL = 3
PLACES_Z, PLACES_Y = 8, 4
CTX_Z, CTX_Y = 3, 2
CROSS = CTX_Z + CTX_Y
TALL = 2
FIRST_LOCAL, FIRST_CROSS = 3, 6
ROWS = 16
CUM = 11
MSG = DH + 16
NEVER = -1e30


def dot(a, b, dims=((1,), (0,))):
    return lax.dot_general(a, b, (dims, ((), ())), preferred_element_type=F32)


def split(x, terms):
    parts = []
    for _ in range(terms):
        part = x.astype(BF16)
        parts.append(part)
        x = x - part.astype(F32)
    return parts


def kernel(
    tokens, w_query, w_key, w_value, w_out, rates_in, row_index_in, table_in,
    out,
    rates, row_index, table, small_sem,
    tok, wkv, wq, kv, local_states, local_out, cross_lhs, cross_states,
    table_rows, table_parts, rate_rows, cum_rows, offset_rows, send_state, recv_state,
    gathered, other, weights, spare, partial, their_partial, own_partial, staged,
    tok_sem, w_sem, wl_sem, wx_send, wx_recv,
    st_send, st_recv, g_send, g_recv, x_send, x_recv, p_send, p_recv, out_send, out_recv,
):
    pos = lax.axis_index("ctx")
    me = lax.axis_index("head")
    x = lax.div(me, 2)
    core = lax.rem(me, 2)
    pair = x + 1 - 2 * lax.rem(x, 2)
    across = 3 - x
    far = lax.rem(x + 2, 4)
    z = lax.rem(pos, PLACES_Z)
    y = lax.div(pos, PLACES_Z)
    sibling_id = (pos, 2 * x + 1 - core)
    pair_id = (pos, 2 * pair + core)
    across_id = (pos, 2 * across + core)
    far_id = (pos, 2 * far + core)
    z_bits = [lax.rem(lax.div(z, 2**b), 2) for b in range(CTX_Z)]
    flips = [2**b * (1 - 2 * z_bits[b]) for b in range(CTX_Z)]
    state_ids = [(pos + shift, me) for shift in (flips[0], flips[1], flips[1] + flips[2])]
    state_ids += [(lax.rem(y + d, PLACES_Y) * PLACES_Z + z, me) for d in range(1, PLACES_Y)]
    partners = [sibling_id, pair_id, across_id, far_id] + state_ids

    barrier = pltpu.get_barrier_semaphore()
    for partner in partners:
        pl.semaphore_signal(barrier, inc=1, device_id=partner, device_id_type=MESH)

    def weight_copy(source, head, part):
        return pltpu.make_async_copy(
            source.at[:, pl.ds(head * DH, DH)],
            wkv.at[head, :, pl.ds(part * DH, DH)],
            w_sem.at[head * 2 + part],
        )

    def token_rows(u, count):
        return pl.ds(pl.multiple_of(u * CHUNK, CHUNK), count * CHUNK)

    def token_copy(u):
        return pltpu.make_async_copy(
            tokens.at[token_rows(u, 1), :], tok.at[token_rows(u, 1), :], tok_sem.at[u]
        )

    small = [
        pltpu.make_async_copy(source, target, small_sem.at[i])
        for i, (source, target) in enumerate(((rates_in, rates), (row_index_in, row_index), (table_in, table)))
    ]
    for copy in small:
        copy.start()
    query_copy = pltpu.make_async_copy(w_query, wq, w_sem.at[4])
    weight_copy(w_key, 0, 0).start()
    weight_copy(w_value, 0, 1).start()
    for u in range(CHUNKS):
        token_copy(u).start()

    homes = [(weights.at[0], 0, x), (weights.at[0], 1, across), (spare, 0, far), (spare, 1, pair)]
    own_pieces = []
    for i, (buffer, a, chip) in enumerate(homes):
        for k, side in enumerate((core, 1 - core)):
            columns = pl.ds(pl.multiple_of((2 * chip + side) * 256, 256), 256)
            own_pieces.append(
                pltpu.make_async_copy(w_out.at[:, columns], buffer.at[2 * a + k], wl_sem.at[2 * i + k])
            )

    def weight_send(i, source, target_ref, target):
        return pltpu.make_async_remote_copy(
            src_ref=source, dst_ref=target_ref, send_sem=wx_send.at[i],
            recv_sem=wx_recv.at[i], device_id=target, device_id_type=MESH,
        )

    weight_sends = [
        weight_send(0, spare.at[y], weights.at[3, y], far_id),
        weight_send(1, weights.at[0], weights.at[2], across_id),
        weight_send(2, spare, weights.at[1], pair_id),
    ]
    far_sends = [
        weight_send(2 + d, weights.at[3, y], weights.at[3, y], state_ids[CTX_Z + d - 1])
        for d in range(1, PLACES_Y)
    ]

    for copy in small:
        copy.wait()

    for u in range(CHUNKS):
        rate_rows[HEADS * u : HEADS * (u + 1), :] = rates[:, u * CHUNK : (u + 1) * CHUNK]
    before = lax.broadcasted_iota(jnp.int32, (CHUNK, CHUNK), 0)
    after = lax.broadcasted_iota(jnp.int32, (CHUNK, CHUNK), 1)
    upper = (before <= after).astype(BF16)
    cum = sum(dot(part, upper) for part in split(-rate_rows[...], 3))
    cum_rows[...] = cum
    last = cum[:, CHUNK - 1 :]
    key_decay = jnp.exp(last - cum).T
    totals = [[last[HEADS * u + h : HEADS * u + h + 1, :] for u in range(CHUNKS)] for h in range(HEADS)]

    table_rows[...] = jnp.zeros_like(table_rows)
    levels = table.shape[0]
    for h in range(HEADS):
        table_rows[h * ROWS : h * ROWS + levels, :] = table[:, h, :]
    for i, part in enumerate(split(table_rows[...], 3)):
        table_parts[i] = part
    level = lax.broadcasted_iota(jnp.int32, (ROWS, 128), 0)
    none = jnp.zeros((1, 1), F32)
    for u in range(CHUNKS):
        for h in range(HEADS):
            offset = jnp.where(level >= FIRST_CROSS, sum(totals[h][:u], none), none)
            ends = [none, totals[h][u - 1] if u % 2 else none, sum(totals[h][4:u], none)]
            for bit in range(LOCAL):
                end = ends[bit] if (u >> bit) & 1 else NEVER
                offset = jnp.where(level == FIRST_LOCAL + bit, end, offset)
            offset_rows[HEADS * u + h] = offset

    def key_value(h, i):
        result = dot(tok[token_rows(i * TALL, TALL), :], wkv[h]).astype(BF16)
        for part in range(TALL):
            kv[h, i * TALL + part] = result[part * CHUNK : (part + 1) * CHUNK]

    def chunk_state(h, u):
        decay = key_decay[:, HEADS * u + h : HEADS * u + h + 1]
        decayed = (kv[h, u, :, :DH].astype(F32) * decay).astype(BF16)
        return dot(decayed, kv[h, u, :, DH:], ((0,), (0,)))

    def merge(first, second):
        return jnp.exp(second[1]) * first[0] + second[0], first[1] + second[1]

    running = [None] * HEADS
    passed = [jnp.zeros((1, 1), F32) for _ in range(HEADS)]

    def state_copy(h, b):
        return pltpu.make_async_remote_copy(
            src_ref=send_state.at[h, min(b, CTX_Z)], dst_ref=recv_state.at[h, b], send_sem=st_send.at[h, b],
            recv_sem=st_recv.at[h, b], device_id=state_ids[b], device_id_type=MESH,
        )

    def send(h, b):
        state, total = running[h]
        send_state[h, b, 0:DH, :] = state.astype(BF16)
        row = lax.broadcasted_iota(jnp.int32, (16, DH), 0)
        tail = jnp.zeros((16, DH), F32)
        for i, part in enumerate(split(total, 3)):
            tail = jnp.where(row == i, part.astype(F32), tail)
        send_state[h, b, DH:MSG, :] = tail.astype(BF16)
        for step in [b] if b < CTX_Z else range(CTX_Z, CTX_Z + PLACES_Y - 1):
            state_copy(h, step).start()

    def arrived(h, b):
        state_copy(h, b).wait_recv()
        tail = recv_state[h, b, DH:MSG, :].astype(F32)
        return recv_state[h, b, 0:DH, :].astype(F32), tail[0:1, 0:1] + tail[1:2, 0:1] + tail[2:3, 0:1]

    def keep_cross(h, b, state):
        cross_states[h, b * DH : (b + 1) * DH, :] = state.astype(BF16)

    def receive_z(h, b):
        there, there_total = arrived(h, b)
        is_upper = z_bits[b] == 1
        state, total = running[h]
        low = jnp.where(is_upper, there, state)
        high = jnp.where(is_upper, state, there)
        high_total = jnp.where(is_upper, total, there_total)
        running[h] = (jnp.exp(high_total) * low + high, total + there_total)
        send(h, b + 1)
        keep_cross(h, b, jnp.where(is_upper, jnp.exp(passed[h]) * there, 0.0))
        passed[h] = passed[h] + jnp.where(is_upper, there_total, 0.0)

    def receive_y(h):
        behind = [arrived(h, CTX_Z + d) for d in range(PLACES_Y - 1)]
        is_odd, is_upper = lax.rem(y, 2) == 1, lax.div(y, 2) == 1
        (one, one_total), (two, two_total), (three, _) = behind
        keep_cross(h, CTX_Z, jnp.where(is_odd, jnp.exp(passed[h]) * one, 0.0))
        first, second = jnp.where(is_odd, three, two), jnp.where(is_odd, two, one)
        second_total = jnp.where(is_odd, two_total, one_total)
        ahead = passed[h] + jnp.where(is_odd, one_total, 0.0)
        both = jnp.exp(ahead) * (jnp.exp(second_total) * first + second)
        keep_cross(h, CTX_Z + 1, jnp.where(is_upper, both, 0.0))

    def own_state(h):
        single = [(chunk_state(h, u), totals[h][u]) for u in range(CHUNKS)]
        pairs = [merge(single[2 * i], single[2 * i + 1]) for i in range(4)]
        quads = [merge(pairs[2 * i], pairs[2 * i + 1]) for i in range(2)]
        running[h] = merge(quads[0], quads[1])
        send(h, 0)
        zero = jnp.zeros((DH, DH), BF16)
        for u in range(CHUNKS):
            lower = [
                single[u - 1][0].astype(BF16) if u & 1 else zero,
                pairs[u // 2 - 1][0].astype(BF16) if u & 2 else zero,
                quads[0][0].astype(BF16) if u & 4 else zero,
            ]
            for i, state in enumerate(lower):
                local_states[h, u, i * DH : (i + 1) * DH, :] = state

    weight_copy(w_key, 0, 0).wait()
    weight_copy(w_value, 0, 1).wait()

    def first_head(i, carry):
        for part in range(TALL):
            token_copy(i * TALL + part).wait()
        key_value(0, i)
        return carry

    def second_head(i, carry):
        key_value(1, i)
        return carry

    for copy in own_pieces:
        copy.start()
    weight_copy(w_key, 1, 0).start()
    weight_copy(w_value, 1, 1).start()
    query_copy.start()
    lax.fori_loop(0, 1, first_head, 0)
    pl.semaphore_wait(barrier, len(partners))
    lax.fori_loop(1, 3, first_head, 0)
    for copy in own_pieces:
        copy.wait()
    for copy in weight_sends:
        copy.start()
    lax.fori_loop(3, CHUNKS // TALL, first_head, 0)
    own_state(0)

    weight_copy(w_key, 1, 0).wait()
    weight_copy(w_value, 1, 1).wait()
    lax.fori_loop(0, CHUNKS // TALL, second_head, 0)
    receive_z(0, 0)
    own_state(1)
    query_copy.wait()
    weight_sends[0].wait_recv()
    for copy in far_sends:
        copy.start()

    def local_part(u, carry):
        queries = dot(tok[token_rows(u, 1), :], wq[...]).astype(BF16)
        slots = table.shape[2]
        chosen = lax.broadcasted_iota(jnp.int32, (slots, CHUNK), 0) == row_index[:, token_rows(u, 1)]
        chosen = jnp.where(chosen, 1.0, 0.0).astype(BF16)
        level_mix = sum(dot(table_parts[i], chosen) for i in range(3))
        row = lax.broadcasted_iota(jnp.int32, (ROWS, CHUNK), 0)
        rows = []
        for h in range(HEADS):
            cum_row = cum_rows[pl.ds(HEADS * u + h, 1), :]
            decay = cum_row + offset_rows[HEADS * u + h][:, 0:1]
            factor = jnp.exp(jnp.where(row >= FIRST_LOCAL, decay, 0.0))
            scaled = level_mix[h * ROWS : (h + 1) * ROWS, :] * factor
            rows.append(jnp.where(row == CUM, cum_row, scaled))
        cols = jnp.concatenate(rows, axis=0).T
        cols16 = cols.astype(BF16)
        token = lax.broadcasted_iota(jnp.int32, (CHUNK, CHUNK), 0)
        source = lax.broadcasted_iota(jnp.int32, (CHUNK, CHUNK), 1)
        causal = token >= source
        same_block = lax.div(token, 64) == lax.div(source, 64)
        same_pair = lax.div(token, 128) == lax.div(source, 128)
        for h in range(HEADS):
            column = lambda row: cols[:, h * ROWS + row : h * ROWS + row + 1]
            query = queries[:, h * DH : (h + 1) * DH]
            key, value = kv[h, u, :, 0:DH], kv[h, u, :, DH : 2 * DH]
            gap = column(CUM) - cum_rows[pl.ds(HEADS * u + h, 1), :]
            decay = jnp.exp(jnp.where(causal, gap, NEVER))
            mix = jnp.where(same_block, column(0), jnp.where(same_pair, column(1), column(2)))
            scores = dot(query, key, ((1,), (1,)))
            result = dot((scores * decay * mix).astype(BF16), value)
            column16 = lambda row: cols16[:, h * ROWS + row : h * ROWS + row + 1]
            lhs = [query * column16(FIRST_LOCAL + i) for i in range(LOCAL)]
            result += dot(jnp.concatenate(lhs, axis=1), local_states[h, u])
            local_out[u, :, h * DH : (h + 1) * DH] = result
            for i in range(CROSS):
                cross_lhs[u, h, :, i * DH : (i + 1) * DH] = query * column16(FIRST_CROSS + i)
        return carry

    lax.fori_loop(0, 2, local_part, 0)
    receive_z(0, 1)
    receive_z(1, 0)
    lax.fori_loop(2, 5, local_part, 0)
    receive_z(0, 2)
    receive_z(1, 1)
    lax.fori_loop(5, CHUNKS, local_part, 0)

    mine = lax.div(x, 2)

    def moved(kind, source, target_slot, target):
        def copy(j, h):
            return pltpu.make_async_remote_copy(
                src_ref=other.at[j, h] if source is None else gathered.at[j, h, source],
                dst_ref=gathered.at[j, h, target_slot], send_sem=g_send.at[kind, j, h],
                recv_sem=g_recv.at[kind, j, h], device_id=target, device_id_type=MESH,
            )

        return copy

    own_to_pair = moved(0, 0, 1, pair_id)
    other_to_across = moved(1, None, 2, across_id)
    across_to_pair = moved(2, 2, 3, pair_id)

    def moved_extra(kind, piece, source, target_slot, target):
        def copy(h):
            return pltpu.make_async_remote_copy(
                src_ref=gathered.at[piece, h, source], dst_ref=gathered.at[EXTRA, h, target_slot],
                send_sem=x_send.at[kind, h], recv_sem=x_recv.at[kind, h],
                device_id=target, device_id_type=MESH,
            )

        return copy

    extra_to_pair = moved_extra(0, EXTRA, 0, 1, pair_id)
    last_to_across = moved_extra(1, LAST, 0, 2, across_id)
    last_pair_to_across = moved_extra(2, LAST, 1, 3, across_id)
    extra_moves = (extra_to_pair, last_to_across, last_pair_to_across)

    def partial_to_sibling(j):
        return pltpu.make_async_remote_copy(
            src_ref=partial.at[j], dst_ref=their_partial.at[j], send_sem=p_send.at[j],
            recv_sem=p_recv.at[j], device_id=sibling_id, device_id_type=MESH,
        )

    def mine_rows(j):
        return pl.ds(pl.multiple_of((mine * PIECES + j) * PIECE, PIECE), PIECE)

    def result_to_across(j):
        return pltpu.make_async_remote_copy(
            src_ref=staged.at[j], dst_ref=out.at[mine_rows(j), :], send_sem=out_send.at[j],
            recv_sem=out_recv.at[j], device_id=across_id, device_id_type=MESH,
        )

    def normed(u, h):
        value = local_out[u, :, h * DH : (h + 1) * DH] + dot(cross_lhs[u, h], cross_states[h])
        square = jnp.mean(value * value, axis=1, keepdims=True)
        return (value * lax.rsqrt(square + EPSILON)).astype(BF16)

    def finish(h):
        def step(j, carry):
            theirs = normed((1 - mine) * HALF + j, h)
            for part in range(CHUNK // PIECE):
                here = j * (CHUNK // PIECE) + part
                other[here, h] = theirs[part * PIECE : (part + 1) * PIECE]
                other_to_across(here, h).start()
            ours = normed(mine * HALF + j, h)
            for part in range(CHUNK // PIECE):
                here = j * (CHUNK // PIECE) + part
                gathered[here, h, 0] = ours[part * PIECE : (part + 1) * PIECE]
                if h == 0:
                    own_to_pair(here, h).start()
            return carry

        lax.fori_loop(0, HALF, step, 0)
        gathered[EXTRA, h, 0] = other[LAST, h]
        last_to_across(h).start()
        if h == 1:
            own_to_pair(LAST, h).start()

    receive_z(1, 2)
    receive_y(0)
    finish(0)
    receive_y(1)
    finish(1)

    for_own, for_across = (0, 1, 1, 0), (1, 0, 0, 1)

    def forward(j):
        @pl.when(j < LAST)
        def _():
            own_to_pair(j, 1).start()

        for h in range(HEADS):
            other_to_across(j, h).wait_recv()
            across_to_pair(j, h).start()

        @pl.when(j == LAST)
        def _():
            for h in range(HEADS):
                extra_to_pair(h).start()
                own_to_pair(LAST, h).wait_recv()
                last_pair_to_across(h).start()

    def product(j, a, k):
        def term(r):
            both = jnp.concatenate([gathered[j, h, r] for h in range(HEADS)], axis=1)
            return dot(both, weights[r, 2 * a[r] + k])

        return sum(term(r) for r in range(4))

    def project(j):
        for h in range(HEADS):
            own_to_pair(j, h).wait_recv()
            across_to_pair(j, h).wait_recv()
        for i, a in enumerate((for_across, for_own)):
            partial[j, i] = product(j, a, 1).astype(BF16)
        partial_to_sibling(j).start()
        for i, a in enumerate((for_across, for_own)):
            own_partial[j, i] = product(j, a, 0)

    def deliver(j):
        partial_to_sibling(j).wait_recv()
        staged[j] = (own_partial[j, 0] + their_partial[j, 0].astype(F32)).astype(BF16)
        result_to_across(j).start()
        out[mine_rows(j), :] = (own_partial[j, 1] + their_partial[j, 1].astype(F32)).astype(BF16)

    def step(j, carry):
        @pl.when(j < PIECES)
        def _():
            forward(j)

        @pl.when(j == LAG)
        def _():
            for copy in weight_sends[1:] + far_sends:
                copy.wait_recv()

        @pl.when((j >= LAG) & (j < LAST + LAG))
        def _():
            project(j - LAG)

        @pl.when(j > LAG)
        def _():
            deliver(j - LAG - 1)

        return carry

    lax.fori_loop(0, LAST + LAG + 1, step, 0)

    for h in range(HEADS):
        last_to_across(h).wait_recv()
        last_pair_to_across(h).wait_recv()
        across_to_pair(LAST, h).wait_recv()
        extra_to_pair(h).wait_recv()
    for i, piece in enumerate((EXTRA, LAST)):
        partial[LAST, i] = product(piece, for_own, 1).astype(BF16)
    partial_to_sibling(LAST).start()
    results = [product(piece, for_own, 0) for piece in (EXTRA, LAST)]
    partial_to_sibling(LAST).wait_recv()
    extra_rows = pl.ds(pl.multiple_of(((1 - mine) * PIECES + LAST) * PIECE, PIECE), PIECE)
    out[extra_rows, :] = (results[0] + their_partial[LAST, 0].astype(F32)).astype(BF16)
    out[mine_rows(LAST), :] = (results[1] + their_partial[LAST, 1].astype(F32)).astype(BF16)

    def drain(j, carry):
        for copy in (own_to_pair, other_to_across, across_to_pair):
            for h in range(HEADS):
                copy(j, h).wait_send()
        partial_to_sibling(j).wait_send()
        return carry

    def drain_results(j, carry):
        result_to_across(j).wait()
        return carry

    lax.fori_loop(0, PIECES, drain, 0)
    lax.fori_loop(0, LAST, drain_results, 0)
    for copy in extra_moves:
        for h in range(HEADS):
            copy(h).wait_send()
    for copy in weight_sends + far_sends:
        copy.wait_send()
    for h in range(HEADS):
        for b in range(CTX_Z + PLACES_Y - 1):
            state_copy(h, b).wait_send()


def shards(tokens, w_query, w_key, w_value, w_out, decay_rate, level_row_index, level_weight_table):
    rows, depth = tokens.shape
    width = w_query.shape[1]
    vmem = functools.partial(pltpu.VMEM)
    dma = pltpu.SemaphoreType.DMA
    hbm, on_chip = pl.BlockSpec(memory_space=pl.ANY), pl.BlockSpec(memory_space=pltpu.VMEM)
    call = pl.pallas_call(
        kernel,
        out_shape=pltpu.VMEM((rows, width), BF16),
        in_specs=[hbm] * 8,
        out_specs=on_chip,
        scratch_shapes=[
            vmem((HEADS, rows), F32),
            vmem((1, rows), jnp.int32),
            vmem(level_weight_table.shape[::-1], F32),
            dma((3,)),
            vmem((rows, depth), BF16),
            vmem((HEADS, depth, 2 * DH), BF16),
            vmem((depth, width), BF16),
            vmem((HEADS, CHUNKS, CHUNK, 2 * DH), BF16),
            vmem((HEADS, CHUNKS, LOCAL * DH, DH), BF16),
            vmem((CHUNKS, CHUNK, width), F32),
            vmem((CHUNKS, HEADS, CHUNK, CROSS * DH), BF16),
            vmem((HEADS, CROSS * DH, DH), BF16),
            vmem((HEADS * ROWS, level_weight_table.shape[0]), F32),
            vmem((3, HEADS * ROWS, level_weight_table.shape[0]), BF16),
            vmem((HEADS * CHUNKS, CHUNK), F32),
            vmem((HEADS * CHUNKS, CHUNK), F32),
            vmem((HEADS * CHUNKS, ROWS, 128), F32),
            vmem((HEADS, CTX_Z + 1, MSG, DH), BF16),
            vmem((HEADS, CTX_Z + PLACES_Y - 1, MSG, DH), BF16),
            vmem((PIECES + 1, HEADS, 4, PIECE, DH), BF16),
            vmem((PIECES, HEADS, PIECE, DH), BF16),
            vmem((4, 4, width, width), BF16),
            vmem((4, width, width), BF16),
            vmem((PIECES, 2, PIECE, width), BF16),
            vmem((PIECES, 2, PIECE, width), BF16),
            vmem((LAST, 2, PIECE, width), F32),
            vmem((LAST, PIECE, width), BF16),
            dma((CHUNKS,)), dma((5,)), dma((8,)), dma((6,)), dma((6,)),
            dma((HEADS, CTX_Z + PLACES_Y - 1)), dma((HEADS, CTX_Z + PLACES_Y - 1)),

            dma((3, PIECES, HEADS)), dma((3, PIECES, HEADS)), dma((3, HEADS)), dma((3, HEADS)),
            dma((PIECES,)), dma((PIECES,)), dma((LAST,)), dma((LAST,)),
        ],
        compiler_params=pltpu.CompilerParams(
            collective_id=0, has_side_effects=True, vmem_limit_bytes=56 * 2**20
        ),
    )
    return call(
        tokens, w_query, w_key, w_value, w_out, decay_rate.T, level_row_index.reshape(1, rows),
        level_weight_table.transpose(2, 1, 0),
    )


def solution(mesh):
    placed = (
        P("ctx", None),
        P(None, "head"),
        P(None, "head"),
        P(None, "head"),
        P("head", None),
        P("ctx", "head"),
        P("ctx"),
        P(None, "head", None),
    )
    return jax.shard_map(
        shards, mesh=mesh, in_specs=placed, out_specs=P("ctx", "head"), check_vma=False
    )
```
